128 devices in a mesh: seq: 8 (over y, z_hi), head: 16 (over x, z_lo, core).
Axes of the slice: x: 4, y: 4, z: 4 (z_hi: 2, z_lo: 2; z = z_hi * 2 + z_lo), core: 2. Of those that a mesh axis runs over, the one named last changes fastest.
Arguments:
- sequence_activity: bfloat16 [2, 4096, 4096], P(None, 'seq', 'head'), may hold values from -6 to 6
- lookup_mapping_tensor: bfloat16 [4096, 16, 768], P(None, 'head'), may hold values from -1 to 1, as said below
- stepsize_mapping_matrix: bfloat16 [4096, 16], P(None, 'head'), may hold values from -0.09375 to 0.09375
- logit_sharpness: float32 [16], P('head'), may hold values from 4 to 120
- adapter_gain_vector: float32 [16, 256], P('head'), may hold values from 0.1 to 1.9
- starting_inner_left_matrix: float32 [16, 256, 512], P('head'), may hold values from -0.375 to 0.375
- starting_inner_right_matrix: float32 [16, 512, 256], P('head'), may hold values from -0.25 to 0.25
- final_mixing_matrix: bfloat16 [16, 256, 4096], P('head'), may hold values from -0.09375 to 0.09375
Outputs:
- mixed: bfloat16 [2, 4096, 4096], P(None, 'seq', 'head')
The draws below stay inside these ranges and needn't reach their ends.
Inputs may be any that keep to these rules, and one draw needn't show every extreme that they name: `lookup_mapping_tensor`: entries of order 1 / sqrt(4096).
All inputs are finite; a program needn't handle non-finite values.
Results may differ from the reference program's by a relative error of at most 0.02.
Values may be sent and summed in bfloat16 or wider, within the bound.
A program may use at most 64 MiB of HBM per device.

```python
import math
import jax
import jax.numpy as jnp
from jax import lax

D = 4096
DH = 256
HID = 512
GROUP = 512
WIN = 2048
NS_STEPS = 3
SEQS = 2
HEADS = 16
L = 4096
N_SEQ = 8


def draw_lookup_mapping_tensor(key, part):
    base = jax.random.truncated_normal(key, -6.0, 6.0, (D, HEADS, 3 * DH), jnp.float32)
    return (base / math.sqrt(D)).astype(jnp.bfloat16)


def draw_logit_sharpness(key, part):
    uniform_part = jax.random.uniform(key, (HEADS,), jnp.float32)
    lower, upper = (4.0, 24.0)
    return jnp.exp(math.log(lower) + uniform_part * (math.log(upper) - math.log(lower))).astype(jnp.float32)


def steps_of(key, extent, cuts, low, top_value):
    factor_of, own = 1.0, jax.random.fold_in(key, 6)
    for dim, parts in cuts:
        steps = jnp.exp(jax.random.uniform(jax.random.fold_in(own, dim), (parts,), jnp.float32, low / len(cuts), top_value / len(cuts)))
        factor_of = factor_of * jnp.repeat(steps, extent[dim] // parts).reshape([-1 if axis == dim else 1 for axis in range(len(extent))])
    return factor_of


def centred(key, shape, scale, most, cuts=(), kind=jnp.bfloat16):
    level = steps_of(key, shape, cuts, -0.22, 0.18) if cuts else 1.0
    result = jax.random.normal(key, shape, jnp.float32) * scale * level
    return jnp.minimum(jnp.maximum(result, -most), most).astype(kind)


def setup_inputs(seed: int = 0) -> dict:
    key_of = jax.random.split(jax.random.key(seed), 9)
    return {
        "sequence_activity": centred(key_of[0], (SEQS, L, D), 1.0, 6.0, ((1, 8), (2, 16))),
        "lookup_mapping_tensor": draw_lookup_mapping_tensor(jax.random.fold_in(key_of[8], 71), 0),
        "stepsize_mapping_matrix": centred(key_of[2], (D, HEADS), D ** -0.5, 0.09375, ((1, 16),)),
        "logit_sharpness": draw_logit_sharpness(jax.random.fold_in(key_of[8], 71), 0),
        "adapter_gain_vector": jnp.clip(1.0 + 0.18 * jax.random.normal(key_of[4], (HEADS, DH), jnp.float32), 0.1, 1.9),
        "starting_inner_left_matrix": centred(key_of[5], (HEADS, DH, HID), DH ** -0.5, 0.375, ((0, 16),), jnp.float32),
        "starting_inner_right_matrix": centred(key_of[6], (HEADS, HID, DH), HID ** -0.5, 0.25, ((0, 16),), jnp.float32),
        "final_mixing_matrix": centred(key_of[7], (HEADS, DH, D), (HEADS * DH) ** -0.5, 0.09375, ((0, 16),)),
    }


update_rate = 0.3

def orthogonalize(update):
    scale = lax.rsqrt(jnp.sum(update * update) + 1e-06)
    current = update * scale
    for sweep in range(NS_STEPS):
        if current.shape[0] <= current.shape[1]:
            gram = jnp.dot(current, current.T, precision=lax.Precision.HIGHEST)
            current = 1.5 * current - 0.5 * jnp.dot(gram, current, precision=lax.Precision.HIGHEST)
        else:
            gram = jnp.dot(current.T, current, precision=lax.Precision.HIGHEST)
            current = 1.5 * current - 0.5 * jnp.dot(current, gram, precision=lax.Precision.HIGHEST)
    return current

def fast_group(weight_in, weight_out, keys, weighted, query_rows):
    in_half = weight_in.astype(jnp.bfloat16)
    out_half = weight_out.astype(jnp.bfloat16)
    hidden = jnp.dot(keys, in_half, preferred_element_type=jnp.float32)
    gating = jax.nn.sigmoid(hidden)
    activated = (hidden * gating).astype(jnp.bfloat16)
    grad_out = jnp.dot(activated.T, weighted, preferred_element_type=jnp.float32)
    backward = jnp.dot(weighted, out_half.T, preferred_element_type=jnp.float32)
    slopes = (backward * gating * (1.0 + hidden * (1.0 - gating))).astype(jnp.bfloat16)
    grad_in = jnp.dot(keys.T, slopes, preferred_element_type=jnp.float32)
    new_in = weight_in + update_rate * orthogonalize(grad_in)
    new_out = weight_out + update_rate * orthogonalize(grad_out)
    query_hidden = jnp.dot(query_rows, new_in.astype(jnp.bfloat16), preferred_element_type=jnp.float32)
    query_act = jax.nn.silu(query_hidden).astype(jnp.bfloat16)
    fast = jnp.dot(query_act, new_out.astype(jnp.bfloat16), preferred_element_type=jnp.float32)
    return (new_in, new_out, fast)

def prepare(projected, rate_col, count_seqs):
    head_dim = projected.shape[1] // 3
    query_rows = projected[:, :head_dim]
    keys = projected[:, head_dim:2 * head_dim]
    values = projected[:, 2 * head_dim:]
    query_norm = (query_rows * lax.rsqrt(lax.optimization_barrier(jnp.sum(query_rows * query_rows, axis=1, keepdims=True)) + 1e-06)).astype(jnp.bfloat16)
    key_norm = (keys * lax.rsqrt(lax.optimization_barrier(jnp.sum(keys * keys, axis=1, keepdims=True)) + 1e-06)).astype(jnp.bfloat16)
    value_half = values.astype(jnp.bfloat16)
    weighted = (jax.nn.softplus(rate_col) * values).astype(jnp.bfloat16)
    return (query_norm.reshape(count_seqs, -1, head_dim), key_norm.reshape(count_seqs, -1, head_dim), value_half.reshape(count_seqs, -1, head_dim), weighted.reshape(count_seqs, -1, head_dim))

def attend_window(query_rows, keys, values, scale, start):
    count = query_rows.shape[1]
    window = keys.shape[1] - count
    scores = scale * jnp.einsum('sqd,skd->sqk', query_rows.astype(jnp.float32), keys.astype(jnp.float32))
    row_pos = lax.broadcasted_iota(jnp.int32, (count, count + window), 0)
    col_pos = lax.broadcasted_iota(jnp.int32, (count, count + window), 1)
    valid = (col_pos >= row_pos) & (col_pos <= row_pos + window) & (col_pos + start >= window)
    scores = jnp.where(valid[None], scores, -1e+30)
    highest = lax.optimization_barrier(jnp.max(scores, axis=2, keepdims=True))
    weights = jnp.exp(scores - highest)
    probs = (weights / lax.optimization_barrier(jnp.sum(weights, axis=2, keepdims=True))).astype(jnp.bfloat16)
    return jnp.einsum('sqk,skd->sqd', probs.astype(jnp.float32), values.astype(jnp.float32))

def combine(attended_output, fast, gain):
    normed = fast * lax.rsqrt(lax.optimization_barrier(jnp.mean(fast * fast, axis=-1, keepdims=True)) + 1e-05) * gain
    return (attended_output + normed).astype(jnp.bfloat16)

def reference(sequence_activity, lookup_mapping_tensor, stepsize_mapping_matrix, logit_sharpness, adapter_gain_vector, starting_inner_left_matrix, starting_inner_right_matrix, final_mixing_matrix):
    flattened = sequence_activity.reshape(SEQS * L, D)

    def one_branch_apply(packed):
        proj_head, rate_head, scale, gain, start_in, start_out = packed
        projected = jnp.dot(flattened, proj_head, preferred_element_type=jnp.float32)
        rate_col = jnp.dot(flattened, rate_head[:, None], preferred_element_type=jnp.float32)
        query_rows, keys, values, weighted = prepare(projected, rate_col, SEQS)
        padding = jnp.zeros((SEQS, WIN, DH), jnp.bfloat16)
        key_pad = jnp.concatenate([padding, keys], axis=1)
        value_pad = jnp.concatenate([padding, values], axis=1)
        state_in = jnp.broadcast_to(start_in, (SEQS,) + start_in.shape)
        state_out = jnp.broadcast_to(start_out, (SEQS,) + start_out.shape)
        pieces = []
        for block in range(N_SEQ):
            lower = block * GROUP
            attended_output = attend_window(query_rows[:, lower:lower + GROUP], key_pad[:, lower:lower + GROUP + WIN], value_pad[:, lower:lower + GROUP + WIN], scale, lower)
            state_in, state_out, fast = jax.vmap(fast_group)(state_in, state_out, keys[:, lower:lower + GROUP], weighted[:, lower:lower + GROUP], query_rows[:, lower:lower + GROUP])
            pieces.append(combine(attended_output, fast, gain))
        return jnp.concatenate(pieces, axis=1)
    number_of_branches = lax.map(one_branch_apply, (jnp.moveaxis(lookup_mapping_tensor, 1, 0), stepsize_mapping_matrix.T, logit_sharpness, adapter_gain_vector, starting_inner_left_matrix, starting_inner_right_matrix))
    stacked = jnp.transpose(number_of_branches, (1, 2, 0, 3)).reshape(SEQS * L, HEADS * DH)
    mixed = jnp.dot(stacked, final_mixing_matrix.reshape(HEADS * DH, D), preferred_element_type=jnp.float32)
    return mixed.astype(jnp.bfloat16).reshape(SEQS, L, D)
```

```python
import functools
import jax
import jax.numpy as jnp
from jax import lax
from jax.experimental import pallas as pl
from jax.experimental.pallas import tpu as pltpu
from jax.sharding import PartitionSpec as P

WIN = 2048
NS_STEPS = 3
UPDATE_RATE = 0.3
LOG2E = 1.4426950408889634
MESH = pl.DeviceIdType.MESH
NT = (((1,), (1,)), ((), ()))
TN = (((0,), (0,)), ((), ()))
NN = (((1,), (0,)), ((), ()))


def mm(a, b, dims=NN):
    return lax.dot_general(a, b, dims, preferred_element_type=jnp.float32)


def half(a):
    return a.astype(jnp.bfloat16)


def sigmoid(a):
    return 0.5 * jnp.tanh(0.5 * a) + 0.5


def unit_scaled(update):
    return update * lax.rsqrt(jnp.sum(update * update) + 1e-06)


def chain_step(state_a, state_b, k, g):
    hidden = mm(k, half(state_a[...]))
    back = mm(g, half(state_b[...]))
    gate = sigmoid(hidden)
    act = half(hidden * gate)
    slopes = half(back * gate * (1.0 + hidden * (1.0 - gate)))
    xa = unit_scaled(mm(k, slopes, TN))
    xb = unit_scaled(mm(g, act, TN))
    for _ in range(NS_STEPS):
        ha, hb = half(xa), half(xb)
        gram_a = half(mm(ha, ha, NT))
        gram_b = half(mm(hb, hb, NT))
        xa = 1.5 * xa - 0.5 * mm(gram_a, ha)
        xb = 1.5 * xb - 0.5 * mm(gram_b, hb)
    state_a[...] += UPDATE_RATE * xa
    state_b[...] += UPDATE_RATE * xb


def column_kernel(
    length, reach,
    scale_ref, gain_ref, q_ref, k_ref, v_ref, g_ref, a0_ref, b0_ref, out_ref,
    kwin, vwin, ck, cg, sent_a, sent_b, got_a, got_b, state_a, state_b, top, total, acc,
    feed_send, feed_k, feed_g, own_sem, win_send, win_k, win_v, w_send, w_recv,
):
    p = lax.axis_index("seq")
    h = lax.axis_index("head")
    core = lax.rem(h, 2)
    owners = (core, 3 - core)
    seqs, group, width = q_ref.shape

    barrier = pltpu.get_barrier_semaphore()
    for d in range(1, length):
        pl.semaphore_signal(
            barrier, inc=1, device_id=(lax.rem(p + d, length), h), device_id_type=MESH
        )
    pl.semaphore_wait(barrier, length - 1)

    def feed(s, which):
        src, dst, sem = ((k_ref, ck, feed_k), (g_ref, cg, feed_g))[which]
        return pltpu.make_async_remote_copy(
            src_ref=src.at[s], dst_ref=dst.at[p],
            send_sem=feed_send.at[s, which], recv_sem=sem.at[p],
            device_id=(owners[s], h), device_id_type=MESH,
        )

    def keep(s, which):
        src, dst = ((k_ref, ck), (g_ref, cg))[which]
        return pltpu.make_async_copy(src.at[s], dst.at[p], own_sem.at[which])

    for s in range(seqs):
        for which in range(2):
            pl.when(p != owners[s])(feed(s, which).start)
            pl.when(p == owners[s])(keep(s, which).start)

    def window(d, which):
        src, dst, sem = ((k_ref, kwin, win_k), (v_ref, vwin, win_v))[which]
        return pltpu.make_async_remote_copy(
            src_ref=src, dst_ref=dst.at[d - 1],
            send_sem=win_send.at[d - 1, which], recv_sem=sem.at[d - 1],
            device_id=(lax.rem(p + d, length), h), device_id_type=MESH,
        )

    for d in range(1, reach + 1):
        for which in range(2):
            pl.when(p + d < length)(window(d, which).start)

    def weights(s, b, which):
        src, dst = ((sent_a, got_a), (sent_b, got_b))[which]
        return pltpu.make_async_remote_copy(
            src_ref=src.at[b], dst_ref=dst.at[s],
            send_sem=w_send.at[which, b], recv_sem=w_recv.at[which, s],
            device_id=(b, h), device_id_type=MESH,
        )

    def chain(s):
        state_a[...] = a0_ref[...]
        state_b[...] = b0_ref[...]

        def turn(b, carry):
            @pl.when(b != p)
            def _():
                for dst, sem in ((ck, feed_k), (cg, feed_g)):
                    pltpu.make_async_remote_copy(
                        src_ref=dst.at[b], dst_ref=dst.at[b],
                        send_sem=feed_send.at[0, 0], recv_sem=sem.at[b],
                        device_id=(b, h), device_id_type=MESH,
                    ).wait_recv()

            @pl.when(b == p)
            def _():
                for which in range(2):
                    keep(s, which).wait()

            chain_step(state_a, state_b, ck[b], cg[b])
            new_a, new_b = half(state_a[...]), half(state_b[...])

            @pl.when(b != p)
            def _():
                sent_a[b] = new_a
                weights(s, b, 0).start()
                sent_b[b] = new_b
                weights(s, b, 1).start()

            @pl.when(b == p)
            def _():
                got_a[s] = new_a
                got_b[s] = new_b

            return carry

        lax.fori_loop(0, length, turn, 0)

    for s in range(seqs):
        pl.when(p == owners[s])(functools.partial(chain, s))

    sharp = scale_ref[0] * LOG2E
    tile = group // 2

    def scores(s, r, keys):
        rows = pl.ds(pl.multiple_of(r * tile, tile), tile)
        return rows, mm(q_ref[s, rows], keys, NT) * sharp

    def first(i, carry):
        s, r = i // 2, i % 2
        rows, sc = scores(s, r, k_ref[s])
        row = lax.broadcasted_iota(jnp.int32, sc.shape, 0) + r * tile
        col = lax.broadcasted_iota(jnp.int32, sc.shape, 1)
        sc = jnp.where(col <= row, sc, -1e30)
        high = jnp.max(sc, axis=1, keepdims=True)
        w = jnp.exp2(sc - high)
        top[s, rows] = high
        total[s, rows] = jnp.sum(w, axis=1, keepdims=True)
        acc[s, rows] = mm(half(w), v_ref[s])
        return carry

    lax.fori_loop(0, 2 * seqs, first, 0)

    def later(d, i, carry):
        s, r = i // 2, i % 2
        rows, sc = scores(s, r, kwin[d - 1, s])
        if d == reach:
            row = lax.broadcasted_iota(jnp.int32, sc.shape, 0) + r * tile
            col = lax.broadcasted_iota(jnp.int32, sc.shape, 1)
            sc = jnp.where(col >= row, sc, -1e30)
        old = top[s, rows]
        high = jnp.maximum(old, jnp.max(sc, axis=1, keepdims=True))
        w = jnp.exp2(sc - high)
        shrink = jnp.exp2(old - high)
        top[s, rows] = high
        total[s, rows] = total[s, rows] * shrink + jnp.sum(w, axis=1, keepdims=True)
        acc[s, rows] = acc[s, rows] * shrink + mm(half(w), vwin[d - 1, s])
        return carry

    for d in range(1, reach + 1):

        @pl.when(p >= d)
        def _():
            for which in range(2):
                window(d, which).wait_recv()
            lax.fori_loop(0, 2 * seqs, functools.partial(later, d), 0)

    for s in range(seqs):

        @pl.when(p != owners[s])
        def _():
            weights(s, p, 0).wait_recv()

        hidden = mm(q_ref[s], got_a[s])
        act = half(hidden * sigmoid(hidden))

        @pl.when(p != owners[s])
        def _():
            weights(s, p, 1).wait_recv()

        fast = mm(act, got_b[s], NT)
        fast = fast * lax.rsqrt(jnp.mean(fast * fast, axis=1, keepdims=True) + 1e-05)
        out_ref[s] = half(acc[s] / total[s] + fast * gain_ref[...])

    for s in range(seqs):
        for which in range(2):
            pl.when(p != owners[s])(feed(s, which).wait_send)
    for d in range(1, reach + 1):
        for which in range(2):
            pl.when(p + d < length)(window(d, which).wait_send)

    @pl.when((p == owners[0]) | (p == owners[1]))
    def _():
        def done(b, carry):
            @pl.when(b != p)
            def _():
                for which in range(2):
                    weights(0, b, which).wait_send()

            return carry

        lax.fori_loop(0, length, done, 0)


def column(scale, gain, q, k, v, g, a0, b0, collective_id):
    seqs, group, width = q.shape
    hid = a0.shape[1]
    length = lax.axis_size("seq")
    reach = WIN // group
    vmem = pl.BlockSpec(memory_space=pltpu.VMEM)
    dma = pltpu.SemaphoreType.DMA
    bf16, f32 = jnp.bfloat16, jnp.float32
    return pl.pallas_call(
        functools.partial(column_kernel, length, reach),
        out_shape=jax.ShapeDtypeStruct(q.shape, bf16),
        in_specs=[pl.BlockSpec(memory_space=pltpu.SMEM)] + [vmem] * 7,
        out_specs=vmem,
        scratch_shapes=[
            pltpu.VMEM((reach, seqs, group, width), bf16),
            pltpu.VMEM((reach, seqs, group, width), bf16),
            pltpu.VMEM((length, group, width), bf16),
            pltpu.VMEM((length, group, width), bf16),
            pltpu.VMEM((length, width, hid), bf16),
            pltpu.VMEM((length, width, hid), bf16),
            pltpu.VMEM((seqs, width, hid), bf16),
            pltpu.VMEM((seqs, width, hid), bf16),
            pltpu.VMEM((width, hid), f32),
            pltpu.VMEM((width, hid), f32),
            pltpu.VMEM((seqs, group, 1), f32),
            pltpu.VMEM((seqs, group, 1), f32),
            pltpu.VMEM((seqs, group, width), f32),
            dma((seqs, 2)), dma((length,)), dma((length,)), dma((2,)),
            dma((reach, 2)), dma((reach,)), dma((reach,)),
            dma((2, length)), dma((2, seqs)),
        ],
        compiler_params=pltpu.CompilerParams(
            collective_id=collective_id, has_side_effects=True, vmem_limit_bytes=48 << 20
        ),
        cost_estimate=pl.CostEstimate(
            flops=10**10, bytes_accessed=10**7, transcendentals=10**6
        ),
    )(scale, gain, q, k, v, g, a0, b0)


def prepare(projected, rate_col, count_seqs):
    head_dim = projected.shape[1] // 3
    query_rows = projected[:, :head_dim]
    keys = projected[:, head_dim : 2 * head_dim]
    values = projected[:, 2 * head_dim :]
    query_norm = (
        query_rows * lax.rsqrt(jnp.sum(query_rows * query_rows, axis=1, keepdims=True) + 1e-06)
    ).astype(jnp.bfloat16)
    key_norm = (keys * lax.rsqrt(jnp.sum(keys * keys, axis=1, keepdims=True) + 1e-06)).astype(
        jnp.bfloat16
    )
    value_half = values.astype(jnp.bfloat16)
    weighted = (jax.nn.softplus(rate_col) * values).astype(jnp.bfloat16)
    return tuple(
        a.reshape(count_seqs, -1, head_dim) for a in (query_norm, key_norm, value_half, weighted)
    )


def body(x, w_in, w_rate, scale, gain, a0, b0, w_out):
    seqs, group, local = x.shape
    rows = seqs * group
    flat = x.reshape(rows, local)
    w_in = w_in.reshape(w_in.shape[0], w_in.shape[2])
    piece = lax.all_gather(flat, "head", axis=1, tiled=True)
    projected = jnp.dot(piece, w_in, preferred_element_type=jnp.float32)
    rate_col = jnp.dot(piece, w_rate, preferred_element_type=jnp.float32)
    q, k, v, g = prepare(projected, rate_col, seqs)
    head_out = column(scale, gain, q, k, v, g, a0[0], b0[0].T, 1)
    head_out = head_out.reshape(rows, -1)
    partial = jnp.dot(head_out, w_out[0], preferred_element_type=jnp.float32)
    result = lax.psum_scatter(
        partial.astype(jnp.bfloat16), "head", scatter_dimension=1, tiled=True
    )
    return result.reshape(seqs, group, -1)


def solution(mesh):
    in_specs = (
        P(None, "seq", "head"),
        P(None, "head", None),
        P(None, "head"),
        P("head"),
        P("head", None),
        P("head", None, None),
        P("head", None, None),
        P("head", None, None),
    )
    out_specs = P(None, "seq", "head")
    return jax.shard_map(body, mesh=mesh, in_specs=in_specs, out_specs=out_specs, check_vma=False)
```

```python
import functools
import jax
import jax.numpy as jnp
from jax import lax
from jax.experimental import pallas as pl
from jax.experimental.pallas import tpu as pltpu
from jax.sharding import PartitionSpec as P

WIN = 2048
NS_STEPS = 3
UPDATE_RATE = 0.3
LOG2E = 1.4426950408889634
MESH = pl.DeviceIdType.MESH
NT = (((1,), (1,)), ((), ()))
TN = (((0,), (0,)), ((), ()))
NN = (((1,), (0,)), ((), ()))


def mm(a, b, dims=NN):
    return lax.dot_general(a, b, dims, preferred_element_type=jnp.float32)


def half(a):
    return a.astype(jnp.bfloat16)


def sigmoid(a):
    return 0.5 * jnp.tanh(0.5 * a) + 0.5


def unit_scaled(update):
    return update * lax.rsqrt(jnp.sum(update * update) + 1e-06)


def chain_step(state_a, state_b, k, g):
    hidden = mm(k, half(state_a[...]))
    back = mm(g, half(state_b[...]))
    gate = sigmoid(hidden)
    act = half(hidden * gate)
    slopes = half(back * gate * (1.0 + hidden * (1.0 - gate)))
    xa = unit_scaled(mm(k, slopes, TN))
    xb = unit_scaled(mm(g, act, TN))
    for _ in range(NS_STEPS):
        ha, hb = half(xa), half(xb)
        gram_a = half(mm(ha, ha, NT))
        gram_b = half(mm(hb, hb, NT))
        xa = 1.5 * xa - 0.5 * mm(gram_a, ha)
        xb = 1.5 * xb - 0.5 * mm(gram_b, hb)
    state_a[...] += UPDATE_RATE * xa
    state_b[...] += UPDATE_RATE * xb


def column_kernel(
    length, reach,
    scale_ref, gain_ref, q_ref, k_ref, v_ref, g_ref, a0_ref, b0_ref, out_ref,
    kwin, vwin, ck, cg, sent_a, sent_b, got_a, got_b, state_a, state_b, top, total, acc,
    feed_send, feed_k, feed_g, own_sem, win_send, win_k, win_v, w_send, w_recv,
):
    p = lax.axis_index("seq")
    h = lax.axis_index("head")
    core = lax.rem(h, 2)
    owners = (core, 3 - core)
    seqs, group, width = q_ref.shape

    barrier = pltpu.get_barrier_semaphore()
    for d in range(1, length):
        pl.semaphore_signal(
            barrier, inc=1, device_id=(lax.rem(p + d, length), h), device_id_type=MESH
        )
    pl.semaphore_wait(barrier, length - 1)

    def feed(s, which):
        src, dst, sem = ((k_ref, ck, feed_k), (g_ref, cg, feed_g))[which]
        return pltpu.make_async_remote_copy(
            src_ref=src.at[s], dst_ref=dst.at[p],
            send_sem=feed_send.at[s, which], recv_sem=sem.at[p],
            device_id=(owners[s], h), device_id_type=MESH,
        )

    def keep(s, which):
        src, dst = ((k_ref, ck), (g_ref, cg))[which]
        return pltpu.make_async_copy(src.at[s], dst.at[p], own_sem.at[which])

    for s in range(seqs):
        for which in range(2):
            pl.when(p != owners[s])(feed(s, which).start)
            pl.when(p == owners[s])(keep(s, which).start)

    def window(d, which):
        src, dst, sem = ((k_ref, kwin, win_k), (v_ref, vwin, win_v))[which]
        return pltpu.make_async_remote_copy(
            src_ref=src, dst_ref=dst.at[d - 1],
            send_sem=win_send.at[d - 1, which], recv_sem=sem.at[d - 1],
            device_id=(lax.rem(p + d, length), h), device_id_type=MESH,
        )

    for d in range(1, reach + 1):
        for which in range(2):
            pl.when(p + d < length)(window(d, which).start)

    def weights(s, b, which):
        src, dst = ((sent_a, got_a), (sent_b, got_b))[which]
        return pltpu.make_async_remote_copy(
            src_ref=src.at[b], dst_ref=dst.at[s],
            send_sem=w_send.at[which, b], recv_sem=w_recv.at[which, s],
            device_id=(b, h), device_id_type=MESH,
        )

    def chain(s):
        state_a[...] = a0_ref[...]
        state_b[...] = b0_ref[...]

        def turn(b, carry):
            @pl.when(b != p)
            def _():
                for dst, sem in ((ck, feed_k), (cg, feed_g)):
                    pltpu.make_async_remote_copy(
                        src_ref=dst.at[b], dst_ref=dst.at[b],
                        send_sem=feed_send.at[0, 0], recv_sem=sem.at[b],
                        device_id=(b, h), device_id_type=MESH,
                    ).wait_recv()

            @pl.when(b == p)
            def _():
                for which in range(2):
                    keep(s, which).wait()

            chain_step(state_a, state_b, ck[b], cg[b])
            new_a, new_b = half(state_a[...]), half(state_b[...])

            @pl.when(b != p)
            def _():
                sent_a[b] = new_a
                weights(s, b, 0).start()
                sent_b[b] = new_b
                weights(s, b, 1).start()

            @pl.when(b == p)
            def _():
                got_a[s] = new_a
                got_b[s] = new_b

            return carry

        lax.fori_loop(0, length, turn, 0)

    for s in range(seqs):
        pl.when(p == owners[s])(functools.partial(chain, s))

    sharp = scale_ref[0] * LOG2E
    tile = group // 2

    def scores(s, r, keys):
        rows = pl.ds(pl.multiple_of(r * tile, tile), tile)
        return rows, mm(q_ref[s, rows], keys, NT) * sharp

    def first(i, carry):
        s, r = i // 2, i % 2
        rows, sc = scores(s, r, k_ref[s])
        row = lax.broadcasted_iota(jnp.int32, sc.shape, 0) + r * tile
        col = lax.broadcasted_iota(jnp.int32, sc.shape, 1)
        sc = jnp.where(col <= row, sc, -1e30)
        high = jnp.max(sc, axis=1, keepdims=True)
        w = jnp.exp2(sc - high)
        top[s, rows] = high
        total[s, rows] = jnp.sum(w, axis=1, keepdims=True)
        acc[s, rows] = mm(half(w), v_ref[s])
        return carry

    lax.fori_loop(0, 2 * seqs, first, 0)

    def later(d, i, carry):
        s, r = i // 2, i % 2
        rows, sc = scores(s, r, kwin[d - 1, s])
        if d == reach:
            row = lax.broadcasted_iota(jnp.int32, sc.shape, 0) + r * tile
            col = lax.broadcasted_iota(jnp.int32, sc.shape, 1)
            sc = jnp.where(col >= row, sc, -1e30)
        old = top[s, rows]
        high = jnp.maximum(old, jnp.max(sc, axis=1, keepdims=True))
        w = jnp.exp2(sc - high)
        shrink = jnp.exp2(old - high)
        top[s, rows] = high
        total[s, rows] = total[s, rows] * shrink + jnp.sum(w, axis=1, keepdims=True)
        acc[s, rows] = acc[s, rows] * shrink + mm(half(w), vwin[d - 1, s])
        return carry

    for d in range(1, reach + 1):

        @pl.when(p >= d)
        def _():
            for which in range(2):
                window(d, which).wait_recv()
            lax.fori_loop(0, 2 * seqs, functools.partial(later, d), 0)

    for s in range(seqs):

        @pl.when(p != owners[s])
        def _():
            weights(s, p, 0).wait_recv()

        hidden = mm(q_ref[s], got_a[s])
        act = half(hidden * sigmoid(hidden))

        @pl.when(p != owners[s])
        def _():
            weights(s, p, 1).wait_recv()

        fast = mm(act, got_b[s], NT)
        fast = fast * lax.rsqrt(jnp.mean(fast * fast, axis=1, keepdims=True) + 1e-05)
        out_ref[s] = half(acc[s] / total[s] + fast * gain_ref[...])

    for s in range(seqs):
        for which in range(2):
            pl.when(p != owners[s])(feed(s, which).wait_send)
    for d in range(1, reach + 1):
        for which in range(2):
            pl.when(p + d < length)(window(d, which).wait_send)

    @pl.when((p == owners[0]) | (p == owners[1]))
    def _():
        def done(b, carry):
            @pl.when(b != p)
            def _():
                for which in range(2):
                    weights(0, b, which).wait_send()

            return carry

        lax.fori_loop(0, length, done, 0)


def column(scale, gain, q, k, v, g, a0, b0, collective_id):
    seqs, group, width = q.shape
    hid = a0.shape[1]
    length = lax.axis_size("seq")
    reach = WIN // group
    vmem = pl.BlockSpec(memory_space=pltpu.VMEM)
    dma = pltpu.SemaphoreType.DMA
    bf16, f32 = jnp.bfloat16, jnp.float32
    return pl.pallas_call(
        functools.partial(column_kernel, length, reach),
        out_shape=jax.ShapeDtypeStruct(q.shape, bf16),
        in_specs=[pl.BlockSpec(memory_space=pltpu.SMEM)] + [vmem] * 7,
        out_specs=vmem,
        scratch_shapes=[
            pltpu.VMEM((reach, seqs, group, width), bf16),
            pltpu.VMEM((reach, seqs, group, width), bf16),
            pltpu.VMEM((length, group, width), bf16),
            pltpu.VMEM((length, group, width), bf16),
            pltpu.VMEM((length, width, hid), bf16),
            pltpu.VMEM((length, width, hid), bf16),
            pltpu.VMEM((seqs, width, hid), bf16),
            pltpu.VMEM((seqs, width, hid), bf16),
            pltpu.VMEM((width, hid), f32),
            pltpu.VMEM((width, hid), f32),
            pltpu.VMEM((seqs, group, 1), f32),
            pltpu.VMEM((seqs, group, 1), f32),
            pltpu.VMEM((seqs, group, width), f32),
            dma((seqs, 2)), dma((length,)), dma((length,)), dma((2,)),
            dma((reach, 2)), dma((reach,)), dma((reach,)),
            dma((2, length)), dma((2, seqs)),
        ],
        compiler_params=pltpu.CompilerParams(
            collective_id=collective_id, has_side_effects=True, vmem_limit_bytes=48 << 20
        ),
        cost_estimate=pl.CostEstimate(
            flops=10**10, bytes_accessed=10**7, transcendentals=10**6
        ),
    )(scale, gain, q, k, v, g, a0, b0)


def gather_kernel(
    finish, n_out, *refs,
):
    x_ref, w_hbm = refs[0], refs[1]
    extra = refs[2:-8 - n_out]
    outs = refs[-8 - n_out:-8]
    held, weights, acc, side, w_sem, send_sem, recv_sem, spare = refs[-8:]
    seq = lax.axis_index("seq")
    me = lax.axis_index("head")
    x, z, core = me // 4, (me // 2) % 2, me % 2

    def at(dx, dz, dc):
        return ((x + dx + 4) % 4) * 4 + ((z + dz) % 2) * 2 + (core + dc) % 2

    plus, minus, across, twin = at(1, 0, 0), at(-1, 0, 0), at(0, 1, 0), at(0, 0, 1)

    load = pltpu.make_async_copy(w_hbm, weights, w_sem)
    load.start()

    barrier = pltpu.get_barrier_semaphore()
    for other in (plus, minus, across, twin):
        pl.semaphore_signal(barrier, inc=1, device_id=(seq, other), device_id_type=MESH)
    pl.semaphore_wait(barrier, 4)

    sends = []

    def send(chunk, t, target, own=False):
        copy = pltpu.make_async_remote_copy(
            src_ref=x_ref.at[t] if own else held.at[chunk, t],
            dst_ref=held.at[chunk, t],
            send_sem=send_sem.at[len(sends)],
            recv_sem=recv_sem.at[chunk, t],
            device_id=(seq, target), device_id_type=MESH,
        )
        copy.start()
        sends.append(copy)

    def arrived(chunk, t):
        pltpu.make_async_remote_copy(
            src_ref=held.at[chunk, t], dst_ref=held.at[chunk, t],
            send_sem=send_sem.at[0], recv_sem=recv_sem.at[chunk, t],
            device_id=(seq, twin), device_id_type=MESH,
        ).wait_recv()

    for i in range(2):
        send(me, i, plus, True)
        send(me, 1 - i, minus, True)
        send(me, i, across, True)
    for i in range(2):
        send(me, i, twin, True)

    finish.init(extra, acc, side)
    load.wait()

    def use(chunk, own=False):
        def step(t, carry):
            block = x_ref[t] if own else held[chunk, t]
            acc[t] += mm(block, weights[chunk])
            finish.each(extra, side, t, chunk, block)
            return carry

        lax.fori_loop(0, 2, step, 0)

    def take(dx, dz, t, targets):
        chunk = at(dx, dz, 0)
        arrived(chunk, t)
        for target in targets:
            send(chunk, t, target)
        send(chunk, t, twin)

    def pair(dx, dz):
        chunk = at(dx, dz, 1)
        for t in range(2):
            arrived(chunk, t)
        use(chunk)

    use(me, True)
    take(-1, 0, 0, (plus,))
    take(1, 0, 1, (minus,))
    take(0, 1, 0, (plus, minus))
    pair(0, 0)
    take(-1, 0, 1, ())
    take(1, 0, 0, ())
    take(0, 1, 1, (plus, minus))
    use(at(-1, 0, 0))
    use(at(1, 0, 0))
    use(at(0, 1, 0))
    pair(-1, 0)
    pair(1, 0)
    pair(0, 1)
    take(2, 0, 0, (across,))
    take(2, 0, 1, (across,))
    use(at(2, 0, 0))
    pair(2, 0)
    take(-1, 1, 0, ())
    take(1, 1, 0, ())
    take(2, 1, 0, ())
    take(-1, 1, 1, ())
    take(1, 1, 1, ())
    use(at(-1, 1, 0))
    use(at(1, 1, 0))
    take(2, 1, 1, ())
    use(at(2, 1, 0))
    pair(-1, 1)
    pair(1, 1)
    pair(2, 1)
    finish.last(extra, acc, side, outs)
    for copy in sends:
        copy.wait_send()


class Projection:
    def init(extra, acc, side):
        acc[...] = jnp.zeros_like(acc)
        side[...] = jnp.zeros_like(side)

    def each(extra, side, t, chunk, block):
        rate = extra[0][chunk]
        lanes = side.shape[2]
        wide = block.astype(jnp.float32)
        total = wide[:, :lanes] * rate[:, :lanes]
        for at in range(lanes, block.shape[1], lanes):
            total += wide[:, at:at + lanes] * rate[:, at:at + lanes]
        side[t] += total

    def last(extra, acc, side, outs):
        width = acc.shape[2] // 3
        for t in range(2):
            q, k, v = (acc[t, :, i * width:(i + 1) * width] for i in range(3))
            rate = jnp.sum(side[t], axis=1, keepdims=True)
            step = jnp.maximum(rate, 0.0) + jnp.log1p(jnp.exp(-jnp.abs(rate)))
            outs[0][t] = half(q * lax.rsqrt(jnp.sum(q * q, axis=1, keepdims=True) + 1e-06))
            outs[1][t] = half(k * lax.rsqrt(jnp.sum(k * k, axis=1, keepdims=True) + 1e-06))
            outs[2][t] = half(v)
            outs[3][t] = half(step * v)


class Mixing:
    def init(extra, acc, side):
        acc[...] = jnp.zeros_like(acc)

    def each(extra, side, t, chunk, block):
        pass

    def last(extra, acc, side, outs):
        outs[0][...] = half(acc[...])


def gather_matmul(x, w, extra, finish, n_out, collective_id):
    seqs, group, local = x.shape
    ways = lax.axis_size("head")
    wide = w.shape[2]
    vmem = pl.BlockSpec(memory_space=pltpu.VMEM)
    dma = pltpu.SemaphoreType.DMA
    out = jax.ShapeDtypeStruct((seqs, group, 256), jnp.bfloat16)
    return pl.pallas_call(
        functools.partial(gather_kernel, finish, n_out),
        out_shape=[out] * n_out,
        in_specs=[vmem, pl.BlockSpec(memory_space=pl.ANY)] + [vmem] * len(extra),
        out_specs=[vmem] * n_out,
        scratch_shapes=[
            pltpu.VMEM((ways, seqs, group, local), jnp.bfloat16),
            pltpu.VMEM(w.shape, jnp.bfloat16),
            pltpu.VMEM((seqs, group, wide), jnp.float32),
            pltpu.VMEM((seqs, group, 128), jnp.float32),
            dma, dma((32,)), dma((ways, 2)), dma,
        ],
        compiler_params=pltpu.CompilerParams(
            collective_id=collective_id, has_side_effects=True, vmem_limit_bytes=40 << 20
        ),
        cost_estimate=pl.CostEstimate(
            flops=2 * seqs * group * ways * local * wide, bytes_accessed=10**7, transcendentals=0
        ),
    )(x, w, *extra)


def body(x, w_in, w_rate, scale, gain, a0, b0, w_out):
    ways = lax.axis_size("head")
    local = x.shape[2]
    w_in = w_in.reshape(ways, local, w_in.shape[2])
    rate = w_rate.astype(jnp.float32).reshape(ways, 1, local)
    pieces = w_out[0].reshape(-1, ways, local).transpose(1, 0, 2)
    q, k, v, g = gather_matmul(x, w_in, (rate,), Projection, 4, 2)
    pieces, q = lax.optimization_barrier((pieces, q))
    mixing = lax.all_to_all(pieces, "head", split_axis=0, concat_axis=0, tiled=True)
    head_out = column(scale, gain, q, k, v, g, a0[0], b0[0].T, 1)
    (out,) = gather_matmul(head_out, mixing, (), Mixing, 1, 3)
    return out


def solution(mesh):
    in_specs = (
        P(None, "seq", "head"),
        P(None, "head", None),
        P(None, "head"),
        P("head"),
        P("head", None),
        P("head", None, None),
        P("head", None, None),
        P("head", None, None),
    )
    out_specs = P(None, "seq", "head")
    return jax.shard_map(body, mesh=mesh, in_specs=in_specs, out_specs=out_specs, check_vma=False)
```

```python
import functools
import jax
import jax.numpy as jnp
from jax import lax
from jax.experimental import pallas as pl
from jax.experimental.pallas import tpu as pltpu
from jax.sharding import PartitionSpec as P

WIN = 2048
NS_STEPS = 3
UPDATE_RATE = 0.3
LOG2E = 1.4426950408889634
MESH = pl.DeviceIdType.MESH
NT = (((1,), (1,)), ((), ()))
TN = (((0,), (0,)), ((), ()))
NN = (((1,), (0,)), ((), ()))


def mm(a, b, dims=NN):
    return lax.dot_general(a, b, dims, preferred_element_type=jnp.float32)


def half(a):
    return a.astype(jnp.bfloat16)


def sigmoid(a):
    return 0.5 * jnp.tanh(0.5 * a) + 0.5


def unit_scaled(update):
    return update * lax.rsqrt(jnp.sum(update * update) + 1e-06)


def chain_step(state_a, state_b, k, g):
    hidden = mm(k, half(state_a[...]))
    back = mm(g, half(state_b[...]))
    gate = sigmoid(hidden)
    act = half(hidden * gate)
    slopes = half(back * gate * (1.0 + hidden * (1.0 - gate)))
    xa = unit_scaled(mm(k, slopes, TN))
    xb = unit_scaled(mm(g, act, TN))
    for _ in range(NS_STEPS):
        ha, hb = half(xa), half(xb)
        gram_a = half(mm(ha, ha, NT))
        gram_b = half(mm(hb, hb, NT))
        xa = 1.5 * xa - 0.5 * mm(gram_a, ha)
        xb = 1.5 * xb - 0.5 * mm(gram_b, hb)
    state_a[...] += UPDATE_RATE * xa
    state_b[...] += UPDATE_RATE * xb


def ring_of(p):
    return p // 2, p % 2


def column_kernel(
    far_owner, late_windows,
    scale_ref, gain_ref, q_ref, k_ref, v_ref, g_ref, a0_ref, b0_ref, w_ref, out_ref, mix_ref,
    kwin, vwin, ck, cg, sent_a, sent_b, got_a, got_b, state_a, state_b, top, total, acc,
    feed_send, feed_k, feed_g, own_sem, win_send, win_k, win_v, w_send, w_recv,
    mix_send, mix_recv, mix_own,
):
    p = lax.axis_index("seq")
    h = lax.axis_index("head")
    y, plane = ring_of(p)
    length = lax.axis_size("seq")
    ways = lax.axis_size("head")
    ring = length // 2
    owner = (h % 2) * far_owner
    pair, group, width = q_ref.shape
    reach = 2

    def place(row):
        return (row % ring) * 2 + plane

    barrier = pltpu.get_barrier_semaphore()
    for d in range(1, ring):
        pl.semaphore_signal(barrier, inc=1, device_id=(place(y + d), h), device_id_type=MESH)
    for d in range(1, ways):
        pl.semaphore_signal(barrier, inc=1, device_id=(p, (h + d) % ways), device_id_type=MESH)
    pl.semaphore_wait(barrier, ring + ways - 2)

    def feed(j, which):
        src, dst, sem = ((k_ref, ck, feed_k), (g_ref, cg, feed_g))[which]
        return pltpu.make_async_remote_copy(
            src_ref=src.at[j], dst_ref=dst.at[2 * y + j],
            send_sem=feed_send.at[j, which], recv_sem=sem.at[2 * y + j],
            device_id=(place(owner), h), device_id_type=MESH,
        )

    def keep(j, which):
        src, dst = ((k_ref, ck), (g_ref, cg))[which]
        return pltpu.make_async_copy(src.at[j], dst.at[2 * y + j], own_sem.at[j, which])

    for j in range(pair):
        for which in range(2):
            pl.when(y != owner)(feed(j, which).start)
            pl.when(y == owner)(keep(j, which).start)

    def window(d, which):
        src, dst, sem = ((k_ref, kwin, win_k), (v_ref, vwin, win_v))[which]
        return pltpu.make_async_remote_copy(
            src_ref=src, dst_ref=dst.at[d - 1],
            send_sem=win_send.at[d - 1, which], recv_sem=sem.at[d - 1],
            device_id=(place(y + d), h), device_id_type=MESH,
        )

    def windows():
        for d in range(1, reach + 1):
            for which in range(2):
                pl.when(y + d < ring)(window(d, which).start)

    def mixing(d):
        other = (h + d) % ways
        return pltpu.make_async_remote_copy(
            src_ref=w_ref.at[:, pl.ds(pl.multiple_of(other * width, width), width)],
            dst_ref=mix_ref.at[h],
            send_sem=mix_send.at[d], recv_sem=mix_recv.at[d],
            device_id=(p, other), device_id_type=MESH,
        )

    mine = pltpu.make_async_copy(
        w_ref.at[:, pl.ds(pl.multiple_of(h * width, width), width)], mix_ref.at[h], mix_own
    )

    if not late_windows:
        windows()
    mine.start()
    for d in range(1, ways):
        mixing(d).start()
    if late_windows:

        @pl.when(y != owner)
        def _():
            for j in range(pair):
                for which in range(2):
                    feed(j, which).wait_send()

        windows()

    def weights(b, which):
        src, dst = ((sent_a, got_a), (sent_b, got_b))[which]
        return pltpu.make_async_remote_copy(
            src_ref=src.at[b], dst_ref=dst.at[b % 2],
            send_sem=w_send.at[which, b], recv_sem=w_recv.at[which, b % 2],
            device_id=(place(b // 2), h), device_id_type=MESH,
        )

    @pl.when(y == owner)
    def _():
        state_a[...] = a0_ref[...]
        state_b[...] = b0_ref[...].T
        for j in range(pair):
            for which in range(2):
                keep(j, which).wait()

        def turn(b, carry):
            @pl.when(b // 2 != y)
            def _():
                for dst, sem in ((ck, feed_k), (cg, feed_g)):
                    pltpu.make_async_remote_copy(
                        src_ref=dst.at[b], dst_ref=dst.at[b],
                        send_sem=feed_send.at[0, 0], recv_sem=sem.at[b],
                        device_id=(place(y + 1), h), device_id_type=MESH,
                    ).wait_recv()

            chain_step(state_a, state_b, ck[b], cg[b])
            new_a, new_b = half(state_a[...]), half(state_b[...])

            @pl.when(b // 2 != y)
            def _():
                sent_a[b] = new_a
                weights(b, 0).start()
                sent_b[b] = new_b
                weights(b, 1).start()

            @pl.when(b // 2 == y)
            def _():
                got_a[b % 2] = new_a
                got_b[b % 2] = new_b

            return carry

        lax.fori_loop(0, length, turn, 0)

    sharp = scale_ref[0] * LOG2E
    tile = group // 2

    def score(j, r, keys, edge):
        rows = pl.ds(pl.multiple_of(r * tile, tile), tile)
        sc = mm(q_ref[j, rows], keys, NT) * sharp
        if edge:
            row = lax.broadcasted_iota(jnp.int32, sc.shape, 0) + r * tile
            col = lax.broadcasted_iota(jnp.int32, sc.shape, 1)
            sc = jnp.where((col <= row) if edge == 1 else (col >= row), sc, -1e30)
        return rows, sc

    def first(i, carry):
        j, r = i // 2, i % 2
        rows, sc = score(j, r, k_ref[j], 1)
        high = jnp.max(sc, axis=1, keepdims=True)
        w = jnp.exp2(sc - high)
        top[j, rows] = high
        total[j, rows] = jnp.sum(w, axis=1, keepdims=True)
        acc[j, rows] = mm(half(w), v_ref[j])
        return carry

    def fold(j, r, keys, values, edge):
        rows, sc = score(j, r, keys, edge)
        old = top[j, rows]
        high = jnp.maximum(old, jnp.max(sc, axis=1, keepdims=True))
        w = jnp.exp2(sc - high)
        shrink = jnp.exp2(old - high)
        top[j, rows] = high
        total[j, rows] = total[j, rows] * shrink + jnp.sum(w, axis=1, keepdims=True)
        acc[j, rows] = acc[j, rows] * shrink + mm(half(w), values)

    lax.fori_loop(0, 2 * pair, first, 0)

    def own(r, carry):
        fold(1, r, k_ref[0], v_ref[0], 0)
        return carry

    lax.fori_loop(0, 2, own, 0)

    @pl.when(y >= 1)
    def _():
        for which in range(2):
            window(1, which).wait_recv()

        def near(i, carry):
            b = i % 2
            fold(i // 4, (i // 2) % 2, kwin[0, b], vwin[0, b], 0)
            return carry

        lax.fori_loop(0, 8, near, 0)

    @pl.when(y >= 2)
    def _():
        for which in range(2):
            window(2, which).wait_recv()

        def edge(i, carry):
            j = i // 2
            fold(j, i % 2, kwin[1, j], vwin[1, j], 2)
            return carry

        lax.fori_loop(0, 4, edge, 0)

        def inner(r, carry):
            fold(0, r, kwin[1, 1], vwin[1, 1], 0)
            return carry

        lax.fori_loop(0, 2, inner, 0)

    for j in range(pair):

        @pl.when(y != owner)
        def _():
            weights(2 * y + j, 0).wait_recv()

        hidden = mm(q_ref[j], got_a[j])
        act = half(hidden * sigmoid(hidden))

        @pl.when(y != owner)
        def _():
            weights(2 * y + j, 1).wait_recv()

        fast = mm(act, got_b[j], NT)
        fast = fast * lax.rsqrt(jnp.mean(fast * fast, axis=1, keepdims=True) + 1e-05)
        out_ref[j] = half(acc[j] / total[j] + fast * gain_ref[...])

    if not late_windows:

        @pl.when(y != owner)
        def _():
            for j in range(pair):
                for which in range(2):
                    feed(j, which).wait_send()

    for d in range(1, reach + 1):
        for which in range(2):
            pl.when(y + d < ring)(window(d, which).wait_send)
    mine.wait()
    for d in range(1, ways):
        mixing(d).wait_send()
        pltpu.make_async_remote_copy(
            src_ref=mix_ref.at[(h - d + ways) % ways], dst_ref=mix_ref.at[(h - d + ways) % ways],
            send_sem=mix_send.at[d], recv_sem=mix_recv.at[d],
            device_id=(p, (h + d) % ways), device_id_type=MESH,
        ).wait_recv()

    @pl.when(y == owner)
    def _():
        def done(b, carry):
            @pl.when(b // 2 != y)
            def _():
                for which in range(2):
                    weights(b, which).wait_send()

            return carry

        lax.fori_loop(0, length, done, 0)


FAR_OWNER = 3
LATE_WINDOWS = False


def column(scale, gain, q, k, v, g, a0, b0, w_out, collective_id):
    pair, group, width = q.shape
    hid = a0.shape[1]
    length = lax.axis_size("seq")
    ways = lax.axis_size("head")
    vmem = pl.BlockSpec(memory_space=pltpu.VMEM)
    dma = pltpu.SemaphoreType.DMA
    bf16, f32 = jnp.bfloat16, jnp.float32
    return pl.pallas_call(
        functools.partial(column_kernel, FAR_OWNER, LATE_WINDOWS),
        out_shape=[
            jax.ShapeDtypeStruct(q.shape, bf16),
            jax.ShapeDtypeStruct((ways, width, width), bf16),
        ],
        in_specs=[pl.BlockSpec(memory_space=pltpu.SMEM)] + [vmem] * 7
        + [pl.BlockSpec(memory_space=pl.ANY)],
        out_specs=[vmem, vmem],
        scratch_shapes=[
            pltpu.VMEM((2, pair, group, width), bf16),
            pltpu.VMEM((2, pair, group, width), bf16),
            pltpu.VMEM((length, group, width), bf16),
            pltpu.VMEM((length, group, width), bf16),
            pltpu.VMEM((length, width, hid), bf16),
            pltpu.VMEM((length, width, hid), bf16),
            pltpu.VMEM((pair, width, hid), bf16),
            pltpu.VMEM((pair, width, hid), bf16),
            pltpu.VMEM((width, hid), f32),
            pltpu.VMEM((width, hid), f32),
            pltpu.VMEM((pair, group, 1), f32),
            pltpu.VMEM((pair, group, 1), f32),
            pltpu.VMEM((pair, group, width), f32),
            dma((pair, 2)), dma((length,)), dma((length,)), dma((pair, 2)),
            dma((2, 2)), dma((2,)), dma((2,)),
            dma((2, length)), dma((2, pair)),
            dma((ways,)), dma((ways,)), dma,
        ],
        compiler_params=pltpu.CompilerParams(
            collective_id=collective_id, has_side_effects=True, vmem_limit_bytes=48 << 20
        ),
        cost_estimate=pl.CostEstimate(
            flops=10**10, bytes_accessed=10**7, transcendentals=10**6
        ),
    )(scale, gain, q, k, v, g, a0, b0, w_out)


def gather_kernel(finish, n_in, n_out, *refs):
    x_ref, w_hbm = refs[:2]
    extra = refs[2:2 + n_in]
    outs = refs[2 + n_in:2 + n_in + n_out]
    held, weights, acc, side, stage, w_sem, send_sem, recv_sem, swap_sem = refs[2 + n_in + n_out:]
    p = lax.axis_index("seq")
    me = lax.axis_index("head")
    y, plane = ring_of(p)
    partner = 2 * y + 1 - plane
    x, z, core = me // 4, (me // 2) % 2, me % 2
    first = plane if finish.inward else 1 - plane

    def at(dx, dz, dc):
        return ((x + dx + 4) % 4) * 4 + ((z + dz) % 2) * 2 + (core + dc) % 2

    plus, minus, across, twin = at(1, 0, 0), at(-1, 0, 0), at(0, 1, 0), at(0, 0, 1)

    load = pltpu.make_async_copy(w_hbm, weights, w_sem)
    load.start()

    barrier = pltpu.get_barrier_semaphore()
    pl.semaphore_signal(barrier, inc=1, device_id=(partner, me), device_id_type=MESH)
    for other in (plus, minus, across, twin):
        pl.semaphore_signal(barrier, inc=1, device_id=(p, other), device_id_type=MESH)
    pl.semaphore_wait(barrier, 5)

    sends = []

    def send(chunk, t, target, source=None):
        copy = pltpu.make_async_remote_copy(
            src_ref=held.at[chunk, t] if source is None else source,
            dst_ref=held.at[chunk, t],
            send_sem=send_sem.at[len(sends)],
            recv_sem=recv_sem.at[chunk, t],
            device_id=target, device_id_type=MESH,
        )
        copy.start()
        sends.append(copy)

    def arrived(chunk, t):
        pltpu.make_async_remote_copy(
            src_ref=held.at[chunk, t], dst_ref=held.at[chunk, t],
            send_sem=send_sem.at[0], recv_sem=recv_sem.at[chunk, t],
            device_id=(p, twin), device_id_type=MESH,
        ).wait_recv()

    if finish.inward:
        send(me, 1, (partner, me), x_ref.at[1 - first])
    for other in (plus, minus, across, twin):
        send(me, 0, (p, other), x_ref.at[first])
    if not finish.inward:
        for other in (minus, plus, across, twin):
            send(me, 1, (p, other), x_ref.at[1 - first])
        held[me, 1] = x_ref[1 - first]
    held[me, 0] = x_ref[first]

    acc[...] = jnp.zeros_like(acc)
    finish.start(side)
    load.wait()

    def take(dx, dz, t, targets):
        chunk = at(dx, dz, 0)
        arrived(chunk, t)
        for target in targets:
            send(chunk, t, (p, target))
        send(chunk, t, (p, twin))

    def use(dx, dz, t):
        here, there = at(dx, dz, 0), at(dx, dz, 1)
        arrived(there, t)

        def step(i, carry):
            chunk = here + i * (there - here)
            block = held[chunk, t]
            acc[t] += mm(block, weights[chunk])
            finish.each(extra, side, t, chunk, block)
            return carry

        lax.fori_loop(0, 2, step, 0)

    take(-1, 0, 0, (plus,))
    take(0, 1, 0, (plus, minus))
    take(1, 0, 0, ())
    if finish.inward:
        arrived(me, 1)
        for other in (minus, plus, across, twin):
            send(me, 1, (p, other))
    use(0, 0, 0)
    use(-1, 0, 0)
    use(0, 1, 0)
    use(1, 0, 0)
    take(1, 0, 1, (minus,))
    take(0, 1, 1, (minus, plus))
    take(-1, 0, 1, ())
    take(2, 0, 0, (across,))
    use(0, 0, 1)
    use(2, 0, 0)
    take(-1, 1, 0, ())
    take(1, 1, 0, ())
    use(1, 0, 1)
    use(0, 1, 1)
    use(-1, 0, 1)
    take(2, 0, 1, (across,))
    take(2, 1, 0, ())
    use(-1, 1, 0)
    use(1, 1, 0)
    use(2, 1, 0)
    back = None
    if not finish.inward:
        stage[...] = half(acc[0])
        back = pltpu.make_async_remote_copy(
            src_ref=stage, dst_ref=outs[0].at[plane],
            send_sem=swap_sem.at[0], recv_sem=swap_sem.at[1],
            device_id=(partner, me), device_id_type=MESH,
        )
        back.start()
    use(2, 0, 1)
    take(-1, 1, 1, ())
    take(1, 1, 1, ())
    take(2, 1, 1, ())
    use(-1, 1, 1)
    use(1, 1, 1)
    use(2, 1, 1)
    if finish.inward:
        for t in range(2):
            finish.last(acc, side, outs, t, t + first - 2 * t * first)
    else:
        outs[0][plane] = half(acc[1])
        back.wait()
    for copy in sends:
        copy.wait_send()


class Projection:
    inward = True

    def start(side):
        side[...] = jnp.zeros_like(side)

    def each(extra, side, t, chunk, block):
        rate = extra[0][chunk]
        lanes = side.shape[2]
        wide = block.astype(jnp.float32)
        total = wide[:, :lanes] * rate[:, :lanes]
        for at in range(lanes, block.shape[1], lanes):
            total += wide[:, at:at + lanes] * rate[:, at:at + lanes]
        side[t] += total

    def last(acc, side, outs, t, row):
        width = acc.shape[2] // 3
        q, k, v = (acc[t, :, i * width:(i + 1) * width] for i in range(3))
        rate = jnp.sum(side[t], axis=1, keepdims=True)
        step = jnp.maximum(rate, 0.0) + jnp.log1p(jnp.exp(-jnp.abs(rate)))
        outs[0][row] = half(q * lax.rsqrt(jnp.sum(q * q, axis=1, keepdims=True) + 1e-06))
        outs[1][row] = half(k * lax.rsqrt(jnp.sum(k * k, axis=1, keepdims=True) + 1e-06))
        outs[2][row] = half(v)
        outs[3][row] = half(step * v)


class Mixing:
    inward = False

    def start(side):
        pass

    def each(extra, side, t, chunk, block):
        pass


def gather_matmul(x, w, extra, finish, n_out, limit, collective_id):
    pair, group, local = x.shape
    ways = lax.axis_size("head")
    wide = w.shape[2]
    vmem = pl.BlockSpec(memory_space=pltpu.VMEM)
    dma = pltpu.SemaphoreType.DMA
    out = jax.ShapeDtypeStruct((pair, group, 256), jnp.bfloat16)
    return pl.pallas_call(
        functools.partial(gather_kernel, finish, len(extra), n_out),
        out_shape=[out] * n_out,
        in_specs=[vmem, pl.BlockSpec(memory_space=pl.ANY)] + [vmem] * len(extra),
        out_specs=[vmem] * n_out,
        scratch_shapes=[
            pltpu.VMEM((ways, 2, group, local), jnp.bfloat16),
            pltpu.VMEM(w.shape, jnp.bfloat16),
            pltpu.VMEM((2, group, wide), jnp.float32),
            pltpu.VMEM((2, group, 128), jnp.float32),
            pltpu.VMEM((group, 256), jnp.bfloat16),
            dma, dma((40,)), dma((ways, 2)), dma((2,)),
        ],
        compiler_params=pltpu.CompilerParams(
            collective_id=collective_id, has_side_effects=True, vmem_limit_bytes=limit << 20
        ),
        cost_estimate=pl.CostEstimate(
            flops=2 * pair * group * ways * local * wide, bytes_accessed=10**7, transcendentals=0
        ),
    )(x, w, *extra)


def body(x, w_in, w_rate, scale, gain, a0, b0, w_out):
    ways = lax.axis_size("head")
    local = x.shape[2]
    w_in = w_in.reshape(ways, local, w_in.shape[2])
    rate = w_rate.astype(jnp.float32).reshape(ways, 1, local)
    q, k, v, g = gather_matmul(x, w_in, (rate,), Projection, 4, 50, 2)
    head_out, mixing = column(scale, gain, q, k, v, g, a0[0], b0[0], w_out[0], 1)
    (out,) = gather_matmul(head_out, mixing, (), Mixing, 1, 32, 3)
    return out


def solution(mesh):
    in_specs = (
        P(None, "seq", "head"),
        P(None, "head", None),
        P(None, "head"),
        P("head"),
        P("head", None),
        P("head", None, None),
        P("head", None, None),
        P("head", None, None),
    )
    out_specs = P(None, "seq", "head")
    return jax.shard_map(body, mesh=mesh, in_specs=in_specs, out_specs=out_specs, check_vma=False)
```

```python
import functools
import jax
import jax.numpy as jnp
from jax import lax
from jax.experimental import pallas as pl
from jax.experimental.pallas import tpu as pltpu
from jax.sharding import PartitionSpec as P

WIN = 2048
NS_STEPS = 3
UPDATE_RATE = 0.3
LOG2E = 1.4426950408889634
MESH = pl.DeviceIdType.MESH
NT = (((1,), (1,)), ((), ()))
TN = (((0,), (0,)), ((), ()))
NN = (((1,), (0,)), ((), ()))


def mm(a, b, dims=NN):
    return lax.dot_general(a, b, dims, preferred_element_type=jnp.float32)


def half(a):
    return a.astype(jnp.bfloat16)


def sigmoid(a):
    return 0.5 * jnp.tanh(0.5 * a) + 0.5


def unit_scaled(update):
    return update * lax.rsqrt(jnp.sum(update * update) + 1e-06)


def chain_step(state_a, state_b, k, g):
    hidden = mm(k, half(state_a[...]))
    back = mm(g, half(state_b[...]))
    gate = sigmoid(hidden)
    act = half(hidden * gate)
    slopes = half(back * gate * (1.0 + hidden * (1.0 - gate)))
    xa = unit_scaled(mm(k, slopes, TN))
    xb = unit_scaled(mm(g, act, TN))
    for _ in range(NS_STEPS):
        ha, hb = half(xa), half(xb)
        gram_a = half(mm(ha, ha, NT))
        gram_b = half(mm(hb, hb, NT))
        xa = 1.5 * xa - 0.5 * mm(gram_a, ha)
        xb = 1.5 * xb - 0.5 * mm(gram_b, hb)
    state_a[...] += UPDATE_RATE * xa
    state_b[...] += UPDATE_RATE * xb


def ring_of(p):
    return p // 2, p % 2


def front_kernel(
    scale_ref, gain_ref, x_ref, w_hbm, rate_ref, a0_ref, b0_ref, w_ref, out_ref, mix_ref,
    held, weights, pacc, side, q_ref, k_ref, v_ref, t_ref, kwin, vwin, twin_ref,
    state_a, state_b, top, total, acc,
    w_sem, send_sem, recv_sem, out_sem, win_sem, mix_send, mix_recv, mix_own,
):
    p = lax.axis_index("seq")
    h = lax.axis_index("head")
    y, plane = ring_of(p)
    ways = lax.axis_size("head")
    ring = lax.axis_size("seq") // 2
    pair, group, width = q_ref.shape
    early, late = plane, 1 - plane

    def place(row):
        return ((row + ring) % ring) * 2 + plane

    load = pltpu.make_async_copy(w_hbm, weights, w_sem)
    load.start()
    barrier = pltpu.get_barrier_semaphore()
    pl.semaphore_signal(barrier, inc=1, device_id=(2 * y + 1 - plane, h), device_id_type=MESH)
    for d in range(1, ways):
        pl.semaphore_signal(barrier, inc=1, device_id=(p, (h + d) % ways), device_id_type=MESH)
    for d in range(1, ring):
        pl.semaphore_signal(barrier, inc=1, device_id=(place(y + d), h), device_id_type=MESH)
    pl.semaphore_wait(barrier, ways + ring - 1)

    pieces = ((k_ref, kwin), (v_ref, vwin), (t_ref, twin_ref))
    to_next, to_back, relayed = 0, 1, 2

    def outgoing(site, j, which, src, target, slot):
        return pltpu.make_async_remote_copy(
            src_ref=src, dst_ref=pieces[which][1].at[slot, j],
            send_sem=out_sem.at[site, j, which], recv_sem=win_sem.at[slot, j, which],
            device_id=(place(target), h), device_id_type=MESH,
        )

    def next_copy(j, which):
        return outgoing(to_next, j, which, pieces[which][0].at[j], y + 1, 0)

    def back_copy(j, which):
        return outgoing(to_back, j, which, pieces[which][0].at[j], y - 1, 2)

    def goes_next():
        return y < ring - 1

    def goes_back(j):
        return (y == 0) | ((y == 1) & (j == 0))

    def project(t, row):
        q, k, v = (pacc[t, :, i * width:(i + 1) * width] for i in range(3))
        q_ref[row] = half(q * lax.rsqrt(jnp.sum(q * q, axis=1, keepdims=True) + 1e-06))
        k_ref[row] = half(k * lax.rsqrt(jnp.sum(k * k, axis=1, keepdims=True) + 1e-06))
        v_ref[row] = half(v)
        rate = jnp.sum(side[t], axis=1, keepdims=True)
        step = jnp.maximum(rate, 0.0) + jnp.log1p(jnp.exp(-jnp.abs(rate)))
        t_ref[row] = jnp.broadcast_to(step, (group, 128)).T[:8]
        for which in range(3):
            pl.when(goes_back(row))(back_copy(row, which).start)
            pl.when(goes_next())(next_copy(row, which).start)

    def each(t, chunk, block):
        rate = rate_ref[chunk]
        wide = block.astype(jnp.float32)
        part = wide[:, :128] * rate[:, :128]
        for at in range(128, width, 128):
            part += wide[:, at:at + 128] * rate[:, at:at + 128]
        side[t] += part

    side[...] = jnp.zeros_like(side)
    gather(
        p, h, plane, early, True, x_ref, held, weights, pacc, load, send_sem, recv_sem,
        each, lambda: project(0, early),
    )
    project(1, late)

    def mixing(d):
        other = (h + d) % ways
        return pltpu.make_async_remote_copy(
            src_ref=w_ref.at[:, pl.ds(pl.multiple_of(other * width, width), width)],
            dst_ref=mix_ref.at[h],
            send_sem=mix_send.at[d], recv_sem=mix_recv.at[d],
            device_id=(p, other), device_id_type=MESH,
        )

    mine = pltpu.make_async_copy(
        w_ref.at[:, pl.ds(pl.multiple_of(h * width, width), width)], mix_ref.at[h], mix_own
    )
    mine.start()
    for d in range(1, ways):
        mixing(d).start()

    state_a[...] = a0_ref[...]
    state_b[...] = b0_ref[...].T

    sharp = scale_ref[0] * LOG2E
    tile = group // 2

    def score(j, r, keys, edge):
        rows = pl.ds(pl.multiple_of(r * tile, tile), tile)
        sc = mm(q_ref[j, rows], keys, NT) * sharp
        if edge:
            row = lax.broadcasted_iota(jnp.int32, sc.shape, 0) + r * tile
            col = lax.broadcasted_iota(jnp.int32, sc.shape, 1)
            sc = jnp.where((col <= row) if edge == 1 else (col >= row), sc, -1e30)
        return rows, sc

    def first(i, carry):
        j, r = i // 2, i % 2
        rows, sc = score(j, r, k_ref[j], 1)
        high = jnp.max(sc, axis=1, keepdims=True)
        w = jnp.exp2(sc - high)
        top[j, rows] = high
        total[j, rows] = jnp.sum(w, axis=1, keepdims=True)
        acc[j, rows] = mm(half(w), v_ref[j])
        return carry

    def fold(j, r, keys, values, edge):
        rows, sc = score(j, r, keys, edge)
        old = top[j, rows]
        high = jnp.maximum(old, jnp.max(sc, axis=1, keepdims=True))
        w = jnp.exp2(sc - high)
        shrink = jnp.exp2(old - high)
        top[j, rows] = high
        total[j, rows] = total[j, rows] * shrink + jnp.sum(w, axis=1, keepdims=True)
        acc[j, rows] = acc[j, rows] * shrink + mm(half(w), values)

    def arrive(slot, j):
        for which in range(3):
            pltpu.make_async_remote_copy(
                src_ref=pieces[which][1].at[slot, j], dst_ref=pieces[which][1].at[slot, j],
                send_sem=out_sem.at[0, 0, which], recv_sem=win_sem.at[slot, j, which],
                device_id=(place(y + 1), h), device_id_type=MESH,
            ).wait_recv()

    def relay(slot, j, target):
        for which in range(3):
            outgoing(relayed, j, which, pieces[which][1].at[slot, j], target, 1).start()

    def learn(k, v, t):
        steps = t.T[:, :1]
        chain_step(state_a, state_b, k, half(v.astype(jnp.float32) * steps))

    def learn_pair(slot):
        def turn(j, carry):
            learn(kwin[slot, j], vwin[slot, j], twin_ref[slot, j])
            return carry

        lax.fori_loop(0, pair, turn, 0)

    def near(b):
        def turn(i, carry):
            fold(i // 2, i % 2, kwin[0, b], vwin[0, b], 0)
            return carry

        lax.fori_loop(0, 2 * pair, turn, 0)

    lax.fori_loop(0, 2 * pair, first, 0)

    def own(r, carry):
        fold(1, r, k_ref[0], v_ref[0], 0)
        return carry

    lax.fori_loop(0, 2, own, 0)

    @pl.when(y == 0)
    def _():
        arrive(2, 0)
        relay(2, 0, y - 1)

    @pl.when(y == 2)
    def _():
        arrive(0, 1)
        relay(0, 1, y + 1)
        arrive(0, 0)

    @pl.when(y == 3)
    def _():
        arrive(2, early)
        relay(2, early, y - 1)

    @pl.when((y == 1) | (y == 3))
    def _():
        arrive(0, early)

    pl.when(y >= 1)(lambda: near(early))

    @pl.when(y == 3)
    def _():
        arrive(2, late)
        relay(2, late, y - 1)
        learn_pair(2)

    @pl.when(y >= 2)
    def _():
        arrive(1, 0)
        arrive(1, 1)

        def edge(i, carry):
            j = i // 2
            fold(j, i % 2, kwin[1, j], vwin[1, j], 2)
            return carry

        lax.fori_loop(0, 4, edge, 0)

        def inner(r, carry):
            fold(0, r, kwin[1, 1], vwin[1, 1], 0)
            return carry

        lax.fori_loop(0, 2, inner, 0)
        learn_pair(1)

    @pl.when((y == 1) | (y == 3))
    def _():
        arrive(0, late)

    @pl.when(y >= 1)
    def _():
        near(late)
        learn_pair(0)

    def answer(j, carry):
        learn(k_ref[j], v_ref[j], t_ref[j])
        hidden = mm(q_ref[j], half(state_a[...]))
        act = half(hidden * sigmoid(hidden))
        fast = mm(act, half(state_b[...]), NT)
        fast = fast * lax.rsqrt(jnp.mean(fast * fast, axis=1, keepdims=True) + 1e-05)
        out_ref[j] = half(acc[j] / total[j] + fast * gain_ref[...])
        return carry

    lax.fori_loop(0, pair, answer, 0)

    for j in range(pair):
        for which in range(3):
            pl.when(goes_next())(next_copy(j, which).wait_send)
            pl.when(goes_back(j))(back_copy(j, which).wait_send)
            moved = (y == 3) | ((y == 0) & (j == 0)) | ((y == 2) & (j == 1))
            pl.when(moved)(
                outgoing(relayed, j, which, pieces[which][1].at[2, j], y - 1, 1).wait_send
            )
    mine.wait()
    for d in range(1, ways):
        mixing(d).wait_send()
        source = (h - d + ways) % ways
        pltpu.make_async_remote_copy(
            src_ref=mix_ref.at[source], dst_ref=mix_ref.at[source],
            send_sem=mix_send.at[d], recv_sem=mix_recv.at[d],
            device_id=(p, (h + d) % ways), device_id_type=MESH,
        ).wait_recv()


def front(scale, gain, x, w_in, rate, a0, b0, w_out, collective_id):
    pair, group, width = x.shape
    hid = a0.shape[1]
    ways = lax.axis_size("head")
    ring = lax.axis_size("seq") // 2
    vmem = pl.BlockSpec(memory_space=pltpu.VMEM)
    hbm = pl.BlockSpec(memory_space=pl.ANY)
    dma = pltpu.SemaphoreType.DMA
    bf16, f32 = jnp.bfloat16, jnp.float32
    block = pltpu.VMEM((pair, group, width), bf16)
    window = pltpu.VMEM((ring - 1, pair, group, width), bf16)
    return pl.pallas_call(
        front_kernel,
        out_shape=[
            jax.ShapeDtypeStruct(x.shape, bf16),
            jax.ShapeDtypeStruct((ways, width, width), bf16),
        ],
        in_specs=[pl.BlockSpec(memory_space=pltpu.SMEM), vmem, vmem, hbm, vmem, vmem, vmem, hbm],
        out_specs=[vmem, vmem],
        scratch_shapes=[
            pltpu.VMEM((ways, pair, group, width), bf16),
            pltpu.VMEM(w_in.shape, bf16),
            pltpu.VMEM((pair, group, w_in.shape[2]), f32),
            pltpu.VMEM((pair, group, 128), f32),
            block, block, block,
            pltpu.VMEM((pair, 8, group), f32),
            window, window,
            pltpu.VMEM((ring - 1, pair, 8, group), f32),
            pltpu.VMEM((width, hid), f32),
            pltpu.VMEM((width, hid), f32),
            pltpu.VMEM((pair, group, 1), f32),
            pltpu.VMEM((pair, group, 1), f32),
            pltpu.VMEM((pair, group, width), f32),
            dma, dma((40,)), dma((ways, 2)),
            dma((3, pair, 3)), dma((ring - 1, pair, 3)),
            dma((ways,)), dma((ways,)), dma,
        ],
        compiler_params=pltpu.CompilerParams(
            collective_id=collective_id, has_side_effects=True, vmem_limit_bytes=50 << 20
        ),
        cost_estimate=pl.CostEstimate(
            flops=2 * 10**10, bytes_accessed=10**7, transcendentals=10**6
        ),
    )(scale, gain, x, w_in, rate, a0, b0, w_out)


def gather(
    p, me, plane, first, inward, x_ref, held, weights, acc, load, send_sem, recv_sem, each, middle
):
    partner = 2 * (p // 2) + 1 - plane
    x, z, core = me // 4, (me // 2) % 2, me % 2

    def at(dx, dz, dc):
        return ((x + dx + 4) % 4) * 4 + ((z + dz) % 2) * 2 + (core + dc) % 2

    plus, minus, across, twin = at(1, 0, 0), at(-1, 0, 0), at(0, 1, 0), at(0, 0, 1)
    sends = []

    def send(chunk, t, target, source=None):
        copy = pltpu.make_async_remote_copy(
            src_ref=held.at[chunk, t] if source is None else source,
            dst_ref=held.at[chunk, t],
            send_sem=send_sem.at[len(sends)],
            recv_sem=recv_sem.at[chunk, t],
            device_id=target, device_id_type=MESH,
        )
        copy.start()
        sends.append(copy)

    def arrived(chunk, t):
        pltpu.make_async_remote_copy(
            src_ref=held.at[chunk, t], dst_ref=held.at[chunk, t],
            send_sem=send_sem.at[0], recv_sem=recv_sem.at[chunk, t],
            device_id=(p, twin), device_id_type=MESH,
        ).wait_recv()

    if inward:
        send(me, 1, (partner, me), x_ref.at[1 - first])
    for other in (plus, minus, across, twin):
        send(me, 0, (p, other), x_ref.at[first])
    if not inward:
        for other in (minus, plus, across, twin):
            send(me, 1, (p, other), x_ref.at[1 - first])
        held[me, 1] = x_ref[1 - first]
    held[me, 0] = x_ref[first]

    acc[...] = jnp.zeros_like(acc)
    load.wait()

    def take(dx, dz, t, targets):
        chunk = at(dx, dz, 0)
        arrived(chunk, t)
        for target in targets:
            send(chunk, t, (p, target))
        send(chunk, t, (p, twin))

    def use(dx, dz, t):
        here, there = at(dx, dz, 0), at(dx, dz, 1)
        arrived(there, t)

        def step(i, carry):
            chunk = here + i * (there - here)
            block = held[chunk, t]
            acc[t] += mm(block, weights[chunk])
            each(t, chunk, block)
            return carry

        lax.fori_loop(0, 2, step, 0)

    take(-1, 0, 0, (plus,))
    take(0, 1, 0, (plus, minus))
    take(1, 0, 0, ())
    if inward:
        arrived(me, 1)
        for other in (minus, plus, across, twin):
            send(me, 1, (p, other))
    use(0, 0, 0)
    use(-1, 0, 0)
    use(0, 1, 0)
    use(1, 0, 0)
    take(1, 0, 1, (minus,))
    take(0, 1, 1, (minus, plus))
    take(-1, 0, 1, ())
    take(2, 0, 0, (across,))
    use(0, 0, 1)
    use(2, 0, 0)
    take(-1, 1, 0, ())
    take(1, 1, 0, ())
    use(1, 0, 1)
    use(0, 1, 1)
    use(-1, 0, 1)
    take(2, 0, 1, (across,))
    take(2, 1, 0, ())
    use(-1, 1, 0)
    use(1, 1, 0)
    use(2, 1, 0)
    middle()
    use(2, 0, 1)
    take(-1, 1, 1, ())
    take(1, 1, 1, ())
    take(2, 1, 1, ())
    use(-1, 1, 1)
    use(1, 1, 1)
    use(2, 1, 1)
    for copy in sends:
        copy.wait_send()


def mixing_kernel(
    x_ref, w_hbm, out_ref, held, weights, acc, stage, w_sem, send_sem, recv_sem, swap_sem
):
    p = lax.axis_index("seq")
    me = lax.axis_index("head")
    y, plane = ring_of(p)
    partner = 2 * y + 1 - plane

    load = pltpu.make_async_copy(w_hbm, weights, w_sem)
    load.start()
    barrier = pltpu.get_barrier_semaphore()
    pl.semaphore_signal(barrier, inc=1, device_id=(partner, me), device_id_type=MESH)
    x, z, core = me // 4, (me // 2) % 2, me % 2
    for other in (
        ((x + 1) % 4) * 4 + z * 2 + core, ((x + 3) % 4) * 4 + z * 2 + core,
        x * 4 + (1 - z) * 2 + core, x * 4 + z * 2 + 1 - core,
    ):
        pl.semaphore_signal(barrier, inc=1, device_id=(p, other), device_id_type=MESH)
    pl.semaphore_wait(barrier, 5)

    back = pltpu.make_async_remote_copy(
        src_ref=stage, dst_ref=out_ref.at[plane],
        send_sem=swap_sem.at[0], recv_sem=swap_sem.at[1],
        device_id=(partner, me), device_id_type=MESH,
    )

    def middle():
        stage[...] = half(acc[0])
        back.start()

    gather(
        p, me, plane, 1 - plane, False, x_ref, held, weights, acc, load, send_sem, recv_sem,
        lambda t, chunk, block: None, middle,
    )
    out_ref[plane] = half(acc[1])
    back.wait()


def mix(x, w, collective_id):
    pair, group, local = x.shape
    ways, _, wide = w.shape
    vmem = pl.BlockSpec(memory_space=pltpu.VMEM)
    dma = pltpu.SemaphoreType.DMA
    return pl.pallas_call(
        mixing_kernel,
        out_shape=jax.ShapeDtypeStruct((pair, group, wide), jnp.bfloat16),
        in_specs=[vmem, pl.BlockSpec(memory_space=pl.ANY)],
        out_specs=vmem,
        scratch_shapes=[
            pltpu.VMEM((ways, pair, group, local), jnp.bfloat16),
            pltpu.VMEM(w.shape, jnp.bfloat16),
            pltpu.VMEM((pair, group, wide), jnp.float32),
            pltpu.VMEM((group, wide), jnp.bfloat16),
            dma, dma((40,)), dma((ways, 2)), dma((2,)),
        ],
        compiler_params=pltpu.CompilerParams(
            collective_id=collective_id, has_side_effects=True, vmem_limit_bytes=32 << 20
        ),
        cost_estimate=pl.CostEstimate(
            flops=2 * pair * group * ways * local * wide, bytes_accessed=10**7, transcendentals=0
        ),
    )(x, w)


def body(x, w_in, w_rate, scale, gain, a0, b0, w_out):
    ways = lax.axis_size("head")
    local = x.shape[2]
    w_in = w_in.reshape(ways, local, w_in.shape[2])
    rate = w_rate.astype(jnp.float32).reshape(ways, 1, local)
    head_out, mixing = front(scale, gain, x, w_in, rate, a0[0], b0[0], w_out[0], 1)
    return mix(head_out, mixing, 2)


def solution(mesh):
    in_specs = (
        P(None, "seq", "head"),
        P(None, "head", None),
        P(None, "head"),
        P("head"),
        P("head", None),
        P("head", None, None),
        P("head", None, None),
        P("head", None, None),
    )
    out_specs = P(None, "seq", "head")
    return jax.shard_map(body, mesh=mesh, in_specs=in_specs, out_specs=out_specs, check_vma=False)
```

```python
import functools
import jax
import jax.numpy as jnp
from jax import lax
from jax.experimental import pallas as pl
from jax.experimental.pallas import tpu as pltpu
from jax.sharding import PartitionSpec as P

WIN = 2048
NS_STEPS = 3
UPDATE_RATE = 0.3
SPLIT_IN = 2
SPLIT_OUT = 1
LOG2E = 1.4426950408889634
MESH = pl.DeviceIdType.MESH
NT = (((1,), (1,)), ((), ()))
TN = (((0,), (0,)), ((), ()))
NN = (((1,), (0,)), ((), ()))


def mm(a, b, dims=NN):
    return lax.dot_general(a, b, dims, preferred_element_type=jnp.float32)


def half(a):
    return a.astype(jnp.bfloat16)


def sigmoid(a):
    return 0.5 * jnp.tanh(0.5 * a) + 0.5


def unit_scaled(update):
    return update * lax.rsqrt(jnp.sum(update * update) + 1e-06)


def chain_step(state_a, state_b, k, g):
    hidden = mm(k, half(state_a[...]))
    back = mm(g, half(state_b[...]))
    gate = sigmoid(hidden)
    act = half(hidden * gate)
    slopes = half(back * gate * (1.0 + hidden * (1.0 - gate)))
    xa = unit_scaled(mm(k, slopes, TN))
    xb = unit_scaled(mm(g, act, TN))
    for _ in range(NS_STEPS):
        ha, hb = half(xa), half(xb)
        gram_a = half(mm(ha, ha, NT))
        gram_b = half(mm(hb, hb, NT))
        xa = 1.5 * xa - 0.5 * mm(gram_a, ha)
        xb = 1.5 * xb - 0.5 * mm(gram_b, hb)
    state_a[...] += UPDATE_RATE * xa
    state_b[...] += UPDATE_RATE * xb


def ring_of(p):
    return p // 2, p % 2


def layer_kernel(
    scale_ref, gain_ref, x_ref, w_hbm, rate_ref, a0_ref, b0_ref, w_ref, out_ref,
    held, weights, pacc, side, q_ref, k_ref, v_ref, t_ref, kwin, vwin, twin_ref,
    state_a, state_b, top, total, acc,
    mix_ref, heads, held_heads, mixed, stage,
    w_sem, send_sem, recv_sem, out_sem, win_sem, mix_send, mix_recv, mix_own,
    send_heads, recv_heads, swap_sem,
):
    p = lax.axis_index("seq")
    h = lax.axis_index("head")
    y, plane = ring_of(p)
    ways = lax.axis_size("head")
    ring = lax.axis_size("seq") // 2
    pair, group, width = q_ref.shape
    early, late = plane, 1 - plane

    def place(row):
        return ((row + ring) % ring) * 2 + plane

    load = pltpu.make_async_copy(w_hbm, weights, w_sem)
    load.start()
    barrier = pltpu.get_barrier_semaphore()
    pl.semaphore_signal(barrier, inc=1, device_id=(2 * y + 1 - plane, h), device_id_type=MESH)
    for d in range(1, ways):
        pl.semaphore_signal(barrier, inc=1, device_id=(p, (h + d) % ways), device_id_type=MESH)
    for d in range(1, ring):
        pl.semaphore_signal(barrier, inc=1, device_id=(place(y + d), h), device_id_type=MESH)
    pl.semaphore_wait(barrier, ways + ring - 1)

    pieces = ((k_ref, kwin), (v_ref, vwin), (t_ref, twin_ref))
    to_next, to_back, relayed = 0, 1, 2

    def outgoing(site, j, which, src, target, slot):
        return pltpu.make_async_remote_copy(
            src_ref=src, dst_ref=pieces[which][1].at[slot, j],
            send_sem=out_sem.at[site, j, which], recv_sem=win_sem.at[slot, j, which],
            device_id=(place(target), h), device_id_type=MESH,
        )

    def next_copy(j, which):
        return outgoing(to_next, j, which, pieces[which][0].at[j], y + 1, 0)

    def back_copy(j, which):
        return outgoing(to_back, j, which, pieces[which][0].at[j], y - 1, 2)

    def goes_next():
        return y < ring - 1

    def goes_back(j):
        return (y == 0) | ((y == 1) & (j == 0))

    def project(t, row):
        q, k, v = (pacc[t, :, i * width:(i + 1) * width] for i in range(3))
        q_ref[row] = half(q * lax.rsqrt(jnp.sum(q * q, axis=1, keepdims=True) + 1e-06))
        k_ref[row] = half(k * lax.rsqrt(jnp.sum(k * k, axis=1, keepdims=True) + 1e-06))
        v_ref[row] = half(v)
        rate = jnp.sum(side[t], axis=1, keepdims=True)
        step = jnp.maximum(rate, 0.0) + jnp.log1p(jnp.exp(-jnp.abs(rate)))
        t_ref[row] = jnp.broadcast_to(step, (group, 128)).T[:8]
        for which in range(3):
            pl.when(goes_back(row))(back_copy(row, which).start)
            pl.when(goes_next())(next_copy(row, which).start)

    def each(t, chunk, block):
        rate = rate_ref[chunk]
        wide = block.astype(jnp.float32)
        part = wide[:, :128] * rate[:, :128]
        for at in range(128, width, 128):
            part += wide[:, at:at + 128] * rate[:, at:at + 128]
        side[t] += part

    side[...] = jnp.zeros_like(side)
    gather(
        p, h, plane, early, True, SPLIT_IN, x_ref, held, weights, pacc, load.wait, send_sem, recv_sem,
        each, lambda: project(0, early),
    )
    project(1, late)

    def mixing(d):
        other = (h + d) % ways
        return pltpu.make_async_remote_copy(
            src_ref=w_ref.at[:, pl.ds(pl.multiple_of(other * width, width), width)],
            dst_ref=mix_ref.at[h],
            send_sem=mix_send.at[d], recv_sem=mix_recv.at[d],
            device_id=(p, other), device_id_type=MESH,
        )

    mine = pltpu.make_async_copy(
        w_ref.at[:, pl.ds(pl.multiple_of(h * width, width), width)], mix_ref.at[h], mix_own
    )
    mine.start()
    for d in range(1, ways):
        mixing(d).start()

    state_a[...] = a0_ref[...]
    state_b[...] = b0_ref[...].T

    sharp = scale_ref[0] * LOG2E
    tile = group // 2

    def score(j, r, keys, edge):
        rows = pl.ds(pl.multiple_of(r * tile, tile), tile)
        sc = mm(q_ref[j, rows], keys, NT) * sharp
        if edge:
            row = lax.broadcasted_iota(jnp.int32, sc.shape, 0) + r * tile
            col = lax.broadcasted_iota(jnp.int32, sc.shape, 1)
            sc = jnp.where((col <= row) if edge == 1 else (col >= row), sc, -1e30)
        return rows, sc

    def first(i, carry):
        j, r = i // 2, i % 2
        rows, sc = score(j, r, k_ref[j], 1)
        high = jnp.max(sc, axis=1, keepdims=True)
        w = jnp.exp2(sc - high)
        top[j, rows] = high
        total[j, rows] = jnp.sum(w, axis=1, keepdims=True)
        acc[j, rows] = mm(half(w), v_ref[j])
        return carry

    def fold(j, r, keys, values, edge):
        rows, sc = score(j, r, keys, edge)
        old = top[j, rows]
        high = jnp.maximum(old, jnp.max(sc, axis=1, keepdims=True))
        w = jnp.exp2(sc - high)
        shrink = jnp.exp2(old - high)
        top[j, rows] = high
        total[j, rows] = total[j, rows] * shrink + jnp.sum(w, axis=1, keepdims=True)
        acc[j, rows] = acc[j, rows] * shrink + mm(half(w), values)

    def arrive(slot, j):
        for which in range(3):
            pltpu.make_async_remote_copy(
                src_ref=pieces[which][1].at[slot, j], dst_ref=pieces[which][1].at[slot, j],
                send_sem=out_sem.at[0, 0, which], recv_sem=win_sem.at[slot, j, which],
                device_id=(place(y + 1), h), device_id_type=MESH,
            ).wait_recv()

    def relay(slot, j, target):
        for which in range(3):
            outgoing(relayed, j, which, pieces[which][1].at[slot, j], target, 1).start()

    def learn(k, v, t):
        steps = t.T[:, :1]
        chain_step(state_a, state_b, k, half(v.astype(jnp.float32) * steps))

    def learn_pair(slot):
        def turn(j, carry):
            learn(kwin[slot, j], vwin[slot, j], twin_ref[slot, j])
            return carry

        lax.fori_loop(0, pair, turn, 0)

    def near(b):
        def turn(i, carry):
            fold(i // 2, i % 2, kwin[0, b], vwin[0, b], 0)
            return carry

        lax.fori_loop(0, 2 * pair, turn, 0)

    lax.fori_loop(0, 2 * pair, first, 0)

    def own(r, carry):
        fold(1, r, k_ref[0], v_ref[0], 0)
        return carry

    lax.fori_loop(0, 2, own, 0)

    @pl.when(y == 0)
    def _():
        arrive(2, 0)
        relay(2, 0, y - 1)

    @pl.when(y == 2)
    def _():
        arrive(0, 1)
        relay(0, 1, y + 1)
        arrive(0, 0)

    @pl.when(y == 3)
    def _():
        arrive(2, early)
        relay(2, early, y - 1)

    @pl.when((y == 1) | (y == 3))
    def _():
        arrive(0, early)

    pl.when(y >= 1)(lambda: near(early))

    @pl.when(y == 3)
    def _():
        arrive(2, late)
        relay(2, late, y - 1)
        learn_pair(2)

    @pl.when((y == 1) | (y == 3))
    def _():
        arrive(0, late)

    pl.when(y >= 1)(lambda: near(late))

    @pl.when(y >= 2)
    def _():
        arrive(1, 0)
        arrive(1, 1)

        def turn(j, carry):
            learn(kwin[1, j], vwin[1, j], twin_ref[1, j])
            for r in range(2):
                fold(j, r, kwin[1, j], vwin[1, j], 2)
            fold(0, j, kwin[1, 1], vwin[1, 1], 0)
            return carry

        lax.fori_loop(0, pair, turn, 0)

    pl.when(y >= 1)(lambda: learn_pair(0))

    def answer(j, carry):
        learn(k_ref[j], v_ref[j], t_ref[j])
        hidden = mm(q_ref[j], half(state_a[...]))
        act = half(hidden * sigmoid(hidden))
        fast = mm(act, half(state_b[...]), NT)
        fast = fast * lax.rsqrt(jnp.mean(fast * fast, axis=1, keepdims=True) + 1e-05)
        heads[j] = half(acc[j] / total[j] + fast * gain_ref[...])
        return carry

    for j in range(pair):
        answer(j, 0)

    def ready():
        mine.wait()
        for d in range(1, ways):
            mixing(d).wait_send()
            source = (h - d + ways) % ways
            pltpu.make_async_remote_copy(
                src_ref=mix_ref.at[source], dst_ref=mix_ref.at[source],
                send_sem=mix_send.at[d], recv_sem=mix_recv.at[d],
                device_id=(p, (h + d) % ways), device_id_type=MESH,
            ).wait_recv()

    back = pltpu.make_async_remote_copy(
        src_ref=stage, dst_ref=out_ref.at[plane],
        send_sem=swap_sem.at[0], recv_sem=swap_sem.at[1],
        device_id=(2 * y + 1 - plane, h), device_id_type=MESH,
    )

    def send_back():
        stage[...] = half(mixed[0])
        back.start()

    gather(
        p, h, plane, 1 - plane, False, SPLIT_OUT, heads, held_heads, mix_ref, mixed, ready,
        send_heads, recv_heads, lambda t, chunk, block: None, send_back,
    )
    out_ref[plane] = half(mixed[1])
    back.wait()
    for j in range(pair):
        for which in range(3):
            pl.when(goes_next())(next_copy(j, which).wait_send)
            pl.when(goes_back(j))(back_copy(j, which).wait_send)
            moved = (y == 3) | ((y == 0) & (j == 0)) | ((y == 2) & (j == 1))
            pl.when(moved)(
                outgoing(relayed, j, which, pieces[which][1].at[2, j], y - 1, 1).wait_send
            )


def layer(scale, gain, x, w_in, rate, a0, b0, w_out, collective_id):
    pair, group, width = x.shape
    hid = a0.shape[1]
    ways = lax.axis_size("head")
    ring = lax.axis_size("seq") // 2
    vmem = pl.BlockSpec(memory_space=pltpu.VMEM)
    hbm = pl.BlockSpec(memory_space=pl.ANY)
    dma = pltpu.SemaphoreType.DMA
    bf16, f32 = jnp.bfloat16, jnp.float32
    block = pltpu.VMEM((pair, group, width), bf16)
    window = pltpu.VMEM((ring - 1, pair, group, width), bf16)
    return pl.pallas_call(
        layer_kernel,
        out_shape=jax.ShapeDtypeStruct(x.shape, bf16),
        in_specs=[pl.BlockSpec(memory_space=pltpu.SMEM), vmem, vmem, hbm, vmem, vmem, vmem, hbm],
        out_specs=vmem,
        scratch_shapes=[
            pltpu.VMEM((ways, pair, group, width), bf16),
            pltpu.VMEM(w_in.shape, bf16),
            pltpu.VMEM((pair, group, w_in.shape[2]), f32),
            pltpu.VMEM((pair, group, 128), f32),
            block, block, block,
            pltpu.VMEM((pair, 8, group), f32),
            window, window,
            pltpu.VMEM((ring - 1, pair, 8, group), f32),
            pltpu.VMEM((width, hid), f32),
            pltpu.VMEM((width, hid), f32),
            pltpu.VMEM((pair, group, 1), f32),
            pltpu.VMEM((pair, group, 1), f32),
            pltpu.VMEM((pair, group, width), f32),
            pltpu.VMEM((ways, width, width), bf16),
            block,
            pltpu.VMEM((ways, pair, group, width), bf16),
            pltpu.VMEM((pair, group, width), f32),
            pltpu.VMEM((group, width), bf16),
            dma, dma((40 * SPLIT_IN,)), dma((ways, 2, SPLIT_IN)),
            dma((3, pair, 3)), dma((ring - 1, pair, 3)),
            dma((ways,)), dma((ways,)), dma,
            dma((40 * SPLIT_OUT,)), dma((ways, 2, SPLIT_OUT)), dma((2,)),
        ],
        compiler_params=pltpu.CompilerParams(
            collective_id=collective_id, has_side_effects=True, vmem_limit_bytes=50 << 20
        ),
        cost_estimate=pl.CostEstimate(
            flops=2 * 10**10, bytes_accessed=10**7, transcendentals=10**6
        ),
    )(scale, gain, x, w_in, rate, a0, b0, w_out)


def gather(
    p, me, plane, first, inward, split, x_ref, held, weights, acc, ready, send_sem, recv_sem, each, middle
):
    partner = 2 * (p // 2) + 1 - plane
    x, z, core = me // 4, (me // 2) % 2, me % 2

    def at(dx, dz, dc):
        return ((x + dx + 4) % 4) * 4 + ((z + dz) % 2) * 2 + (core + dc) % 2

    plus, minus, across, twin = at(1, 0, 0), at(-1, 0, 0), at(0, 1, 0), at(0, 0, 1)
    sends = []

    cut = held.shape[2] // split

    def send(chunk, t, target, source=None, parts=range(split)):
        for u in parts:
            rows = pl.ds(u * cut, cut)
            copy = pltpu.make_async_remote_copy(
                src_ref=held.at[chunk, t, rows] if source is None else source.at[rows],
                dst_ref=held.at[chunk, t, rows],
                send_sem=send_sem.at[len(sends)],
                recv_sem=recv_sem.at[chunk, t, u],
                device_id=target, device_id_type=MESH,
            )
            copy.start()
            sends.append(copy)

    def arrived(chunk, t, parts=range(split)):
        for u in parts:
            rows = pl.ds(u * cut, cut)
            pltpu.make_async_remote_copy(
                src_ref=held.at[chunk, t, rows], dst_ref=held.at[chunk, t, rows],
                send_sem=send_sem.at[0], recv_sem=recv_sem.at[chunk, t, u],
                device_id=(p, twin), device_id_type=MESH,
            ).wait_recv()

    if inward:
        send(me, 1, (partner, me), x_ref.at[1 - first])
    for other in (plus, minus, across, twin):
        send(me, 0, (p, other), x_ref.at[first])
    if not inward:
        for other in (minus, plus, across, twin):
            send(me, 1, (p, other), x_ref.at[1 - first])
        held[me, 1] = x_ref[1 - first]
    held[me, 0] = x_ref[first]

    acc[...] = jnp.zeros_like(acc)
    ready()

    def take(dx, dz, t, targets):
        chunk = at(dx, dz, 0)
        for u in range(split):
            arrived(chunk, t, (u,))
            for target in targets:
                send(chunk, t, (p, target), None, (u,))
            send(chunk, t, (p, twin), None, (u,))

    def use(dx, dz, t):
        here, there = at(dx, dz, 0), at(dx, dz, 1)
        arrived(there, t)

        def step(i, carry):
            chunk = here + i * (there - here)
            block = held[chunk, t]
            acc[t] += mm(block, weights[chunk])
            each(t, chunk, block)
            return carry

        lax.fori_loop(0, 2, step, 0)

    take(-1, 0, 0, (plus,))
    take(0, 1, 0, (plus, minus))
    take(1, 0, 0, ())
    if inward:
        for u in range(split):
            arrived(me, 1, (u,))
            for other in (minus, plus, across, twin):
                send(me, 1, (p, other), None, (u,))
    use(0, 0, 0)
    use(-1, 0, 0)
    use(0, 1, 0)
    use(1, 0, 0)
    take(1, 0, 1, (minus,))
    take(0, 1, 1, (minus, plus))
    take(-1, 0, 1, ())
    take(2, 0, 0, (across,))
    use(0, 0, 1)
    use(2, 0, 0)
    take(-1, 1, 0, ())
    take(1, 1, 0, ())
    use(1, 0, 1)
    use(0, 1, 1)
    use(-1, 0, 1)
    take(2, 0, 1, (across,))
    take(2, 1, 0, ())
    use(-1, 1, 0)
    use(1, 1, 0)
    use(2, 1, 0)
    middle()
    use(2, 0, 1)
    take(-1, 1, 1, ())
    take(1, 1, 1, ())
    take(2, 1, 1, ())
    use(-1, 1, 1)
    use(1, 1, 1)
    use(2, 1, 1)
    for copy in sends:
        copy.wait_send()


def body(x, w_in, w_rate, scale, gain, a0, b0, w_out):
    ways = lax.axis_size("head")
    local = x.shape[2]
    w_in = w_in.reshape(ways, local, w_in.shape[2])
    rate = w_rate.astype(jnp.float32).reshape(ways, 1, local)
    return layer(scale, gain, x, w_in, rate, a0[0], b0[0], w_out[0], 1)


def solution(mesh):
    in_specs = (
        P(None, "seq", "head"),
        P(None, "head", None),
        P(None, "head"),
        P("head"),
        P("head", None),
        P("head", None, None),
        P("head", None, None),
        P("head", None, None),
    )
    out_specs = P(None, "seq", "head")
    return jax.shard_map(body, mesh=mesh, in_specs=in_specs, out_specs=out_specs, check_vma=False)
```

```python
import functools
import jax
import jax.numpy as jnp
from jax import lax
from jax.experimental import pallas as pl
from jax.experimental.pallas import tpu as pltpu
from jax.sharding import PartitionSpec as P

WIN = 2048
NS_STEPS = 3
UPDATE_RATE = 0.3
SPLIT_IN = 2
SPLIT_OUT = 1
LOG2E = 1.4426950408889634
MESH = pl.DeviceIdType.MESH
NT = (((1,), (1,)), ((), ()))
TN = (((0,), (0,)), ((), ()))
NN = (((1,), (0,)), ((), ()))


def mm(a, b, dims=NN):
    return lax.dot_general(a, b, dims, preferred_element_type=jnp.float32)


def half(a):
    return a.astype(jnp.bfloat16)


def sigmoid(a):
    return 0.5 * jnp.tanh(0.5 * a) + 0.5


def unit_scale(update):
    return lax.rsqrt(jnp.sum(update * update) + 1e-06)


def chain_step(state_a, state_b, k, g):
    hidden = mm(k, half(state_a[...]))
    back = mm(g, half(state_b[...]))
    gate = sigmoid(hidden)
    act = half(hidden * gate)
    slopes = half(back * gate * (1.0 + hidden * (1.0 - gate)))
    ua, ub = mm(k, slopes, TN), mm(g, act, TN)
    ha, hb = half(ua), half(ub)
    ga, gb = mm(ha, ha, NT), mm(hb, hb, NT)
    sa, sb = unit_scale(ua), unit_scale(ub)
    xa, xb = ua * sa, ub * sb
    gram_a, gram_b = half(ga * sa * sa), half(gb * sb * sb)
    for i in range(NS_STEPS):
        ha, hb = half(xa), half(xb)
        if i:
            gram_a, gram_b = half(mm(ha, ha, NT)), half(mm(hb, hb, NT))
        xa = 1.5 * xa - 0.5 * mm(gram_a, ha)
        xb = 1.5 * xb - 0.5 * mm(gram_b, hb)
    state_a[...] += UPDATE_RATE * xa
    state_b[...] += UPDATE_RATE * xb


def ring_of(p):
    return p // 2, p % 2


def layer_kernel(
    scale_ref, gain_ref, x_ref, w_hbm, rate_ref, a0_ref, b0_ref, w_ref, out_ref,
    held, weights, pacc, side, q_ref, k_ref, v_ref, t_ref, kwin, vwin, twin_ref,
    state_a, state_b, top, total, acc,
    mix_ref, heads, held_heads, mixed, stage,
    w_sem, send_sem, recv_sem, out_sem, win_sem, mix_send, mix_recv, mix_own,
    send_heads, recv_heads, swap_sem, b_rows, gain_row, fetch_sem,
):
    p = lax.axis_index("seq")
    h = lax.axis_index("head")
    y, plane = ring_of(p)
    ways = lax.axis_size("head")
    ring = lax.axis_size("seq") // 2
    pair, group, width = q_ref.shape
    early, late = plane, 1 - plane

    def place(row):
        return ((row + ring) % ring) * 2 + plane

    load = pltpu.make_async_copy(w_hbm, weights, w_sem)
    load.start()
    fetches = [
        pltpu.make_async_copy(src, dst, fetch_sem.at[i])
        for i, (src, dst) in enumerate(((a0_ref, state_a), (b0_ref, b_rows), (gain_ref, gain_row)))
    ]
    for fetch in fetches:
        fetch.start()
    barrier = pltpu.get_barrier_semaphore()
    pl.semaphore_signal(barrier, inc=1, device_id=(2 * y + 1 - plane, h), device_id_type=MESH)
    for d in range(1, ways):
        pl.semaphore_signal(barrier, inc=1, device_id=(p, (h + d) % ways), device_id_type=MESH)
    for d in range(1, ring):
        pl.semaphore_signal(barrier, inc=1, device_id=(place(y + d), h), device_id_type=MESH)
    pl.semaphore_wait(barrier, ways + ring - 1)

    pieces = ((k_ref, kwin), (v_ref, vwin), (t_ref, twin_ref))
    to_next, to_back, relayed = 0, 1, 2

    def outgoing(site, j, which, src, target, slot):
        return pltpu.make_async_remote_copy(
            src_ref=src, dst_ref=pieces[which][1].at[slot, j],
            send_sem=out_sem.at[site, j, which], recv_sem=win_sem.at[slot, j, which],
            device_id=(place(target), h), device_id_type=MESH,
        )

    def next_copy(j, which):
        return outgoing(to_next, j, which, pieces[which][0].at[j], y + 1, 0)

    def back_copy(j, which):
        return outgoing(to_back, j, which, pieces[which][0].at[j], y - 1, 2)

    def goes_next():
        return y < ring - 1

    def goes_back(j):
        return (y == 0) | ((y == 1) & (j == 0))

    def project(t, row):
        q, k, v = (pacc[t, :, i * width:(i + 1) * width] for i in range(3))
        q_ref[row] = half(q * lax.rsqrt(jnp.sum(q * q, axis=1, keepdims=True) + 1e-06))
        k_ref[row] = half(k * lax.rsqrt(jnp.sum(k * k, axis=1, keepdims=True) + 1e-06))
        v_ref[row] = half(v)
        rate = jnp.sum(side[t], axis=1, keepdims=True)
        step = jnp.maximum(rate, 0.0) + jnp.log1p(jnp.exp(-jnp.abs(rate)))
        t_ref[row] = jnp.broadcast_to(step, (group, 128)).T[:8]
        for which in range(3):
            pl.when(goes_back(row))(back_copy(row, which).start)
            pl.when(goes_next())(next_copy(row, which).start)

    def arrive(slot, j):
        for which in range(3):
            pltpu.make_async_remote_copy(
                src_ref=pieces[which][1].at[slot, j], dst_ref=pieces[which][1].at[slot, j],
                send_sem=out_sem.at[0, 0, which], recv_sem=win_sem.at[slot, j, which],
                device_id=(place(y + 1), h), device_id_type=MESH,
            ).wait_recv()

    def relay(slot, j, target):
        for which in range(3):
            outgoing(relayed, j, which, pieces[which][1].at[slot, j], target, 1).start()

    def relays(j):
        @pl.when((y == 0) & (j == 0))
        def _():
            arrive(2, 0)
            relay(2, 0, y - 1)

        @pl.when((y == 2) & (j == 1))
        def _():
            arrive(0, 1)
            relay(0, 1, y + 1)

        @pl.when(y == 3)
        def _():
            arrive(2, j)
            relay(2, j, y - 1)

    def each(t, chunk, block):
        rate = rate_ref[chunk]
        wide = block.astype(jnp.float32)
        part = wide[:, :128] * rate[:, :128]
        for at in range(128, width, 128):
            part += wide[:, at:at + 128] * rate[:, at:at + 128]
        side[t] += part

    side[...] = jnp.zeros_like(side)
    gather(
        p, h, plane, early, True, SPLIT_IN, x_ref, held, weights, pacc, load.wait, send_sem, recv_sem,
        each, lambda: project(0, early), fetch_sem.at[3],
    )
    project(1, late)

    def mixing(d):
        other = (h + d) % ways
        return pltpu.make_async_remote_copy(
            src_ref=w_ref.at[:, pl.ds(pl.multiple_of(other * width, width), width)],
            dst_ref=mix_ref.at[h],
            send_sem=mix_send.at[d], recv_sem=mix_recv.at[d],
            device_id=(p, other), device_id_type=MESH,
        )

    mine = pltpu.make_async_copy(
        w_ref.at[:, pl.ds(pl.multiple_of(h * width, width), width)], mix_ref.at[h], mix_own
    )
    mine.start()
    for d in range(1, ways):
        mixing(d).start()

    for fetch in fetches:
        fetch.wait()
    state_b[...] = b_rows[...].T

    sharp = scale_ref[0] * LOG2E
    tile = group // 2

    def score(j, r, keys, edge):
        rows = pl.ds(pl.multiple_of(r * tile, tile), tile)
        sc = mm(q_ref[j, rows], keys, NT) * sharp
        if edge:
            row = lax.broadcasted_iota(jnp.int32, sc.shape, 0) + r * tile
            col = lax.broadcasted_iota(jnp.int32, sc.shape, 1)
            sc = jnp.where((col <= row) if edge == 1 else (col >= row), sc, -1e30)
        return rows, sc

    def first(i, carry):
        j, r = i // 2, i % 2
        rows, sc = score(j, r, k_ref[j], 1)
        high = jnp.max(sc, axis=1, keepdims=True)
        w = jnp.exp2(sc - high)
        top[j, rows] = high
        total[j, rows] = jnp.sum(w, axis=1, keepdims=True)
        acc[j, rows] = mm(half(w), v_ref[j])
        return carry

    def fold(j, r, keys, values, edge):
        rows, sc = score(j, r, keys, edge)
        old = top[j, rows]
        high = jnp.maximum(old, jnp.max(sc, axis=1, keepdims=True))
        w = jnp.exp2(sc - high)
        shrink = jnp.exp2(old - high)
        top[j, rows] = high
        total[j, rows] = total[j, rows] * shrink + jnp.sum(w, axis=1, keepdims=True)
        acc[j, rows] = acc[j, rows] * shrink + mm(half(w), values)

    def learn(k, v, t):
        steps = t.T[:, :1]
        chain_step(state_a, state_b, k, half(v.astype(jnp.float32) * steps))

    def learn_pair(slot):
        def turn(j, carry):
            learn(kwin[slot, j], vwin[slot, j], twin_ref[slot, j])
            return carry

        lax.fori_loop(0, pair, turn, 0)

    def near(b):
        def turn(i, carry):
            fold(i // 2, i % 2, kwin[0, b], vwin[0, b], 0)
            return carry

        lax.fori_loop(0, 2 * pair, turn, 0)

    lax.fori_loop(0, 2 * pair, first, 0)
    relays(early)

    def own(r, carry):
        fold(1, r, k_ref[0], v_ref[0], 0)
        return carry

    lax.fori_loop(0, 2, own, 0)

    @pl.when(y < 3)
    def _():
        relays(late)

    @pl.when(y == 2)
    def _():
        arrive(0, 0)

    @pl.when((y == 1) | (y == 3))
    def _():
        arrive(0, early)

    pl.when((y == 1) | (y == 2))(lambda: near(early))

    @pl.when(y == 3)
    def _():
        relays(late)

        def both(j, carry):
            learn(kwin[2, j], vwin[2, j], twin_ref[2, j])
            for r in range(2):
                fold(j, r, kwin[0, early], vwin[0, early], 0)
            return carry

        lax.fori_loop(0, pair, both, 0)

    @pl.when((y == 1) | (y == 3))
    def _():
        arrive(0, late)

    pl.when(y >= 1)(lambda: near(late))

    @pl.when(y >= 2)
    def _():
        arrive(1, 0)
        arrive(1, 1)

        def turn(j, carry):
            learn(kwin[1, j], vwin[1, j], twin_ref[1, j])
            for r in range(2):
                fold(j, r, kwin[1, j], vwin[1, j], 2)
            fold(0, j, kwin[1, 1], vwin[1, 1], 0)
            return carry

        lax.fori_loop(0, pair, turn, 0)

    pl.when(y >= 1)(lambda: learn_pair(0))

    def answer(j, carry):
        learn(k_ref[j], v_ref[j], t_ref[j])
        hidden = mm(q_ref[j], half(state_a[...]))
        act = half(hidden * sigmoid(hidden))
        fast = mm(act, half(state_b[...]), NT)
        fast = fast * lax.rsqrt(jnp.mean(fast * fast, axis=1, keepdims=True) + 1e-05)
        heads[j] = half(acc[j] / total[j] + fast * gain_row[...])
        return carry

    for j in range(pair):
        answer(j, 0)

    def ready():
        mine.wait()
        for d in range(1, ways):
            mixing(d).wait_send()
            source = (h - d + ways) % ways
            pltpu.make_async_remote_copy(
                src_ref=mix_ref.at[source], dst_ref=mix_ref.at[source],
                send_sem=mix_send.at[d], recv_sem=mix_recv.at[d],
                device_id=(p, (h + d) % ways), device_id_type=MESH,
            ).wait_recv()

    back = pltpu.make_async_remote_copy(
        src_ref=stage, dst_ref=out_ref.at[plane],
        send_sem=swap_sem.at[0], recv_sem=swap_sem.at[1],
        device_id=(2 * y + 1 - plane, h), device_id_type=MESH,
    )

    def send_back():
        stage[...] = half(mixed[0])
        back.start()

    gather(
        p, h, plane, 1 - plane, False, SPLIT_OUT, heads, held_heads, mix_ref, mixed, ready,
        send_heads, recv_heads, lambda t, chunk, block: None, send_back,
    )
    out_ref[plane] = half(mixed[1])
    back.wait()
    for j in range(pair):
        for which in range(3):
            pl.when(goes_next())(next_copy(j, which).wait_send)
            pl.when(goes_back(j))(back_copy(j, which).wait_send)
            moved = (y == 3) | ((y == 0) & (j == 0)) | ((y == 2) & (j == 1))
            pl.when(moved)(
                outgoing(relayed, j, which, pieces[which][1].at[2, j], y - 1, 1).wait_send
            )


def layer(scale, gain, x, w_in, rate, a0, b0, w_out, collective_id):
    pair, group, width = x.shape
    hid = a0.shape[1]
    ways = lax.axis_size("head")
    ring = lax.axis_size("seq") // 2
    vmem = pl.BlockSpec(memory_space=pltpu.VMEM)
    hbm = pl.BlockSpec(memory_space=pltpu.HBM)
    dma = pltpu.SemaphoreType.DMA
    bf16, f32 = jnp.bfloat16, jnp.float32
    block = pltpu.VMEM((pair, group, width), bf16)
    window = pltpu.VMEM((ring - 1, pair, group, width), bf16)
    return pl.pallas_call(
        layer_kernel,
        out_shape=jax.ShapeDtypeStruct(x.shape, bf16),
        in_specs=[pl.BlockSpec(memory_space=pltpu.SMEM), hbm, hbm, hbm, vmem, hbm, hbm, hbm],
        out_specs=vmem,
        scratch_shapes=[
            pltpu.VMEM((ways, pair, group, width), bf16),
            pltpu.VMEM(w_in.shape, bf16),
            pltpu.VMEM((pair, group, w_in.shape[2]), f32),
            pltpu.VMEM((pair, group, 128), f32),
            block, block, block,
            pltpu.VMEM((pair, 8, group), f32),
            window, window,
            pltpu.VMEM((ring - 1, pair, 8, group), f32),
            pltpu.VMEM((width, hid), f32),
            pltpu.VMEM((width, hid), f32),
            pltpu.VMEM((pair, group, 1), f32),
            pltpu.VMEM((pair, group, 1), f32),
            pltpu.VMEM((pair, group, width), f32),
            pltpu.VMEM((ways, width, width), bf16),
            block,
            pltpu.VMEM((ways, pair, group, width), bf16),
            pltpu.VMEM((pair, group, width), f32),
            pltpu.VMEM((group, width), bf16),
            dma, dma((40 * SPLIT_IN,)), dma((ways, 2, SPLIT_IN)),
            dma((3, pair, 3)), dma((ring - 1, pair, 3)),
            dma((ways,)), dma((ways,)), dma,
            dma((40 * SPLIT_OUT,)), dma((ways, 2, SPLIT_OUT)), dma((2,)),
            pltpu.VMEM(b0.shape, f32), pltpu.VMEM(gain.shape, f32), dma((4,)),
        ],
        compiler_params=pltpu.CompilerParams(
            collective_id=collective_id, has_side_effects=True, vmem_limit_bytes=62 << 20
        ),
        cost_estimate=pl.CostEstimate(
            flops=2 * 10**10, bytes_accessed=10**7, transcendentals=10**6
        ),
    )(scale, gain, x, w_in, rate, a0, b0, w_out)


def gather(
    p, me, plane, first, inward, split, x_ref, held, weights, acc, ready, send_sem, recv_sem, each, middle, swap_sem=None
):
    partner = 2 * (p // 2) + 1 - plane
    x, z, core = me // 4, (me // 2) % 2, me % 2

    def at(dx, dz, dc):
        return ((x + dx + 4) % 4) * 4 + ((z + dz) % 2) * 2 + (core + dc) % 2

    plus, minus, across, twin = at(1, 0, 0), at(-1, 0, 0), at(0, 1, 0), at(0, 0, 1)
    sends = []

    cut = held.shape[2] // split

    def send(chunk, t, target, source=None, parts=range(split)):
        for u in parts:
            rows = pl.ds(u * cut, cut)
            copy = pltpu.make_async_remote_copy(
                src_ref=held.at[chunk, t, rows] if source is None else source.at[rows],
                dst_ref=held.at[chunk, t, rows],
                send_sem=send_sem.at[len(sends)],
                recv_sem=recv_sem.at[chunk, t, u],
                device_id=target, device_id_type=MESH,
            )
            copy.start()
            sends.append(copy)

    def arrived(chunk, t, parts=range(split)):
        for u in parts:
            rows = pl.ds(u * cut, cut)
            pltpu.make_async_remote_copy(
                src_ref=held.at[chunk, t, rows], dst_ref=held.at[chunk, t, rows],
                send_sem=send_sem.at[0], recv_sem=recv_sem.at[chunk, t, u],
                device_id=(p, twin), device_id_type=MESH,
            ).wait_recv()

    if inward:
        send(me, 1, (partner, me), x_ref.at[1 - first])
    for other in (plus, minus, across, twin):
        send(me, 0, (p, other), x_ref.at[first])
    if not inward:
        for other in (minus, plus, across, twin):
            send(me, 1, (p, other), x_ref.at[1 - first])
        held[me, 1] = x_ref[1 - first]
    if inward:
        own = pltpu.make_async_copy(x_ref.at[first], held.at[me, 0], swap_sem)
        own.start()
    else:
        held[me, 0] = x_ref[first]

    acc[...] = jnp.zeros_like(acc)
    ready()

    def take(dx, dz, t, targets):
        chunk = at(dx, dz, 0)
        for u in range(split):
            arrived(chunk, t, (u,))
            for target in targets:
                send(chunk, t, (p, target), None, (u,))
            send(chunk, t, (p, twin), None, (u,))

    def use(dx, dz, t):
        here, there = at(dx, dz, 0), at(dx, dz, 1)
        arrived(there, t)

        def step(i, carry):
            chunk = here + i * (there - here)
            block = held[chunk, t]
            acc[t] += mm(block, weights[chunk])
            each(t, chunk, block)
            return carry

        lax.fori_loop(0, 2, step, 0)

    take(-1, 0, 0, (plus,))
    take(0, 1, 0, (plus, minus))
    take(1, 0, 0, ())
    if inward:
        own.wait()
        for u in range(split):
            arrived(me, 1, (u,))
            for other in (minus, plus, across, twin):
                send(me, 1, (p, other), None, (u,))
    use(0, 0, 0)
    use(-1, 0, 0)
    use(0, 1, 0)
    use(1, 0, 0)
    take(1, 0, 1, (minus,))
    take(0, 1, 1, (minus, plus))
    take(-1, 0, 1, ())
    take(2, 0, 0, (across,))
    use(0, 0, 1)
    use(2, 0, 0)
    take(-1, 1, 0, ())
    take(1, 1, 0, ())
    use(1, 0, 1)
    use(0, 1, 1)
    use(-1, 0, 1)
    take(2, 0, 1, (across,))
    take(2, 1, 0, ())
    use(-1, 1, 0)
    use(1, 1, 0)
    use(2, 1, 0)
    middle()
    use(2, 0, 1)
    take(-1, 1, 1, ())
    take(1, 1, 1, ())
    take(2, 1, 1, ())
    use(-1, 1, 1)
    use(1, 1, 1)
    use(2, 1, 1)
    for copy in sends:
        copy.wait_send()


def body(x, w_in, w_rate, scale, gain, a0, b0, w_out):
    ways = lax.axis_size("head")
    local = x.shape[2]
    w_in = w_in.reshape(ways, local, w_in.shape[2])
    rate = w_rate.astype(jnp.float32).reshape(ways, 1, local)
    return layer(scale, gain, x, w_in, rate, a0[0], b0[0], w_out[0], 1)


def solution(mesh):
    in_specs = (
        P(None, "seq", "head"),
        P(None, "head", None),
        P(None, "head"),
        P("head"),
        P("head", None),
        P("head", None, None),
        P("head", None, None),
        P("head", None, None),
    )
    out_specs = P(None, "seq", "head")
    return jax.shard_map(body, mesh=mesh, in_specs=in_specs, out_specs=out_specs, check_vma=False)
```

```python
import functools
import jax
import jax.numpy as jnp
from jax import lax
from jax.experimental import pallas as pl
from jax.experimental.pallas import tpu as pltpu
from jax.sharding import PartitionSpec as P

WIN = 2048
NS_STEPS = 3
UPDATE_RATE = 0.3
SPLIT_IN = 2
SPLIT_OUT = 1
LOG2E = 1.4426950408889634
MESH = pl.DeviceIdType.MESH
NT = (((1,), (1,)), ((), ()))
TN = (((0,), (0,)), ((), ()))
NN = (((1,), (0,)), ((), ()))


def mm(a, b, dims=NN):
    return lax.dot_general(a, b, dims, preferred_element_type=jnp.float32)


def half(a):
    return a.astype(jnp.bfloat16)


def sigmoid(a):
    return 0.5 * jnp.tanh(0.5 * a) + 0.5


def unit_scale(update):
    return lax.rsqrt(jnp.sum(update * update) + 1e-06)


def chain_step(state_a, state_b, k, g):
    hidden = mm(k, half(state_a[...]))
    back = mm(g, half(state_b[...]))
    gate = sigmoid(hidden)
    act = half(hidden * gate)
    slopes = half(back * gate * (1.0 + hidden * (1.0 - gate)))
    ua, ub = mm(k, slopes, TN), mm(g, act, TN)
    ha, hb = half(ua), half(ub)
    ga, gb = mm(ha, ha, NT), mm(hb, hb, NT)
    sa, sb = unit_scale(ua), unit_scale(ub)
    xa, xb = ua * sa, ub * sb
    gram_a, gram_b = half(ga * sa * sa), half(gb * sb * sb)
    for i in range(NS_STEPS):
        ha, hb = half(xa), half(xb)
        if i:
            gram_a, gram_b = half(mm(ha, ha, NT)), half(mm(hb, hb, NT))
        xa = 1.5 * xa - 0.5 * mm(gram_a, ha)
        xb = 1.5 * xb - 0.5 * mm(gram_b, hb)
    state_a[...] += UPDATE_RATE * xa
    state_b[...] += UPDATE_RATE * xb


def ring_of(p):
    return p // 2, p % 2


def layer_kernel(
    scale_ref, gain_ref, x_ref, w_hbm, rate_ref, a0_ref, b0_ref, w_ref, out_ref,
    held, weights, pacc, side, q_ref, k_ref, v_ref, t_ref, kwin, vwin, twin_ref,
    state_a, state_b, top, total, acc,
    mix_ref, heads, held_heads, mixed, stage,
    w_sem, send_sem, recv_sem, out_sem, win_sem, mix_send, mix_recv, mix_own,
    send_heads, recv_heads, swap_sem, b_rows, gain_row, fetch_sem,
):
    p = lax.axis_index("seq")
    h = lax.axis_index("head")
    y, plane = ring_of(p)
    ways = lax.axis_size("head")
    ring = lax.axis_size("seq") // 2
    pair, group, width = q_ref.shape
    early, late = plane, 1 - plane

    def place(row):
        return ((row + ring) % ring) * 2 + plane

    load = pltpu.make_async_copy(w_hbm, weights, w_sem)
    load.start()
    fetches = [
        pltpu.make_async_copy(src, dst, fetch_sem.at[i])
        for i, (src, dst) in enumerate(((a0_ref, state_a), (b0_ref, b_rows), (gain_ref, gain_row)))
    ]
    for fetch in fetches:
        fetch.start()
    barrier = pltpu.get_barrier_semaphore()
    pl.semaphore_signal(barrier, inc=1, device_id=(2 * y + 1 - plane, h), device_id_type=MESH)
    for d in range(1, ways):
        pl.semaphore_signal(barrier, inc=1, device_id=(p, (h + d) % ways), device_id_type=MESH)
    for d in range(1, ring):
        pl.semaphore_signal(barrier, inc=1, device_id=(place(y + d), h), device_id_type=MESH)
    pl.semaphore_wait(barrier, ways + ring - 1)

    pieces = ((k_ref, kwin), (v_ref, vwin), (t_ref, twin_ref))
    to_next, to_back, relayed = 0, 1, 2

    def outgoing(site, j, which, src, target, slot):
        return pltpu.make_async_remote_copy(
            src_ref=src, dst_ref=pieces[which][1].at[slot, j],
            send_sem=out_sem.at[site, j, which], recv_sem=win_sem.at[slot, j, which],
            device_id=(place(target), h), device_id_type=MESH,
        )

    def next_copy(j, which):
        return outgoing(to_next, j, which, pieces[which][0].at[j], y + 1, 0)

    def back_copy(j, which):
        return outgoing(to_back, j, which, pieces[which][0].at[j], y - 1, 2)

    def goes_next():
        return y < ring - 1

    def goes_back(j):
        return (y == 0) | ((y == 1) & (j == 0))

    def project(t, row):
        q, k, v = (pacc[t, :, i * width:(i + 1) * width] for i in range(3))
        q_ref[row] = half(q * lax.rsqrt(jnp.sum(q * q, axis=1, keepdims=True) + 1e-06))
        k_ref[row] = half(k * lax.rsqrt(jnp.sum(k * k, axis=1, keepdims=True) + 1e-06))
        v_ref[row] = half(v)
        rate = jnp.sum(side[t], axis=1, keepdims=True)
        step = jnp.maximum(rate, 0.0) + jnp.log1p(jnp.exp(-jnp.abs(rate)))
        t_ref[row] = jnp.broadcast_to(step, (group, 128)).T[:8]
        for which in range(3):
            pl.when(goes_back(row))(back_copy(row, which).start)
        for which in range(3):
            pl.when(goes_next())(next_copy(row, which).start)

    def arrive(slot, j):
        for which in range(3):
            pltpu.make_async_remote_copy(
                src_ref=pieces[which][1].at[slot, j], dst_ref=pieces[which][1].at[slot, j],
                send_sem=out_sem.at[0, 0, which], recv_sem=win_sem.at[slot, j, which],
                device_id=(place(y + 1), h), device_id_type=MESH,
            ).wait_recv()

    def relay(slot, j, target):
        for which in range(3):
            outgoing(relayed, j, which, pieces[which][1].at[slot, j], target, 1).start()

    def relays(j):
        @pl.when((y == 0) & (j == 0))
        def _():
            arrive(2, 0)
            relay(2, 0, y - 1)

        @pl.when((y == 2) & (j == 1))
        def _():
            arrive(0, 1)
            relay(0, 1, y + 1)

        @pl.when(y == 3)
        def _():
            arrive(2, j)
            relay(2, j, y - 1)

    def each(t, chunk, block):
        rate = rate_ref[chunk]
        wide = block.astype(jnp.float32)
        part = wide[:, :128] * rate[:, :128]
        for at in range(128, width, 128):
            part += wide[:, at:at + 128] * rate[:, at:at + 128]
        side[t] += part

    side[...] = jnp.zeros_like(side)
    gather(
        p, h, plane, early, True, SPLIT_IN, x_ref, held, weights, pacc, load.wait, send_sem, recv_sem,
        each, lambda: project(0, early), fetch_sem.at[3],
    )
    project(1, late)

    def mixing(d):
        other = (h + d) % ways
        return pltpu.make_async_remote_copy(
            src_ref=w_ref.at[:, pl.ds(pl.multiple_of(other * width, width), width)],
            dst_ref=mix_ref.at[h],
            send_sem=mix_send.at[d], recv_sem=mix_recv.at[d],
            device_id=(p, other), device_id_type=MESH,
        )

    mine = pltpu.make_async_copy(
        w_ref.at[:, pl.ds(pl.multiple_of(h * width, width), width)], mix_ref.at[h], mix_own
    )
    mine.start()
    for d in range(1, ways):
        mixing(d).start()

    for fetch in fetches:
        fetch.wait()
    state_b[...] = b_rows[...].T

    sharp = scale_ref[0] * LOG2E
    tile = group // 2

    def score(j, r, keys, edge):
        rows = pl.ds(pl.multiple_of(r * tile, tile), tile)
        sc = mm(q_ref[j, rows], keys, NT) * sharp
        if edge:
            row = lax.broadcasted_iota(jnp.int32, sc.shape, 0) + r * tile
            col = lax.broadcasted_iota(jnp.int32, sc.shape, 1)
            sc = jnp.where((col <= row) if edge == 1 else (col >= row), sc, -1e30)
        return rows, sc

    def first(i, carry):
        j, r = i // 2, i % 2
        rows, sc = score(j, r, k_ref[j], 1)
        high = jnp.max(sc, axis=1, keepdims=True)
        w = jnp.exp2(sc - high)
        top[j, rows] = high
        total[j, rows] = jnp.sum(w, axis=1, keepdims=True)
        acc[j, rows] = mm(half(w), v_ref[j])
        return carry

    def fold(j, r, keys, values, edge):
        rows, sc = score(j, r, keys, edge)
        old = top[j, rows]
        high = jnp.maximum(old, jnp.max(sc, axis=1, keepdims=True))
        w = jnp.exp2(sc - high)
        shrink = jnp.exp2(old - high)
        top[j, rows] = high
        total[j, rows] = total[j, rows] * shrink + jnp.sum(w, axis=1, keepdims=True)
        acc[j, rows] = acc[j, rows] * shrink + mm(half(w), values)

    def learn(k, v, t):
        steps = t.T[:, :1]
        chain_step(state_a, state_b, k, half(v.astype(jnp.float32) * steps))

    def learn_pair(slot):
        def turn(j, carry):
            learn(kwin[slot, j], vwin[slot, j], twin_ref[slot, j])
            return carry

        lax.fori_loop(0, pair, turn, 0)

    def near(b):
        def turn(i, carry):
            fold(i // 2, i % 2, kwin[0, b], vwin[0, b], 0)
            return carry

        lax.fori_loop(0, 2 * pair, turn, 0)

    lax.fori_loop(0, 2 * pair, first, 0)
    relays(early)

    def own(r, carry):
        fold(1, r, k_ref[0], v_ref[0], 0)
        return carry

    lax.fori_loop(0, 2, own, 0)

    @pl.when(y < 3)
    def _():
        relays(late)

    @pl.when(y == 2)
    def _():
        arrive(0, 0)

    @pl.when((y == 1) | (y == 3))
    def _():
        arrive(0, early)

    pl.when((y == 1) | (y == 2))(lambda: near(early))

    @pl.when(y == 3)
    def _():
        relays(late)

        def both(j, carry):
            learn(kwin[2, j], vwin[2, j], twin_ref[2, j])
            for r in range(2):
                fold(j, r, kwin[0, early], vwin[0, early], 0)
            return carry

        lax.fori_loop(0, pair, both, 0)

    @pl.when((y == 1) | (y == 3))
    def _():
        arrive(0, late)

    pl.when(y >= 1)(lambda: near(late))

    @pl.when(y >= 2)
    def _():
        arrive(1, 0)
        arrive(1, 1)

        def turn(j, carry):
            learn(kwin[1, j], vwin[1, j], twin_ref[1, j])
            for r in range(2):
                fold(j, r, kwin[1, j], vwin[1, j], 2)
            fold(0, j, kwin[1, 1], vwin[1, 1], 0)
            return carry

        lax.fori_loop(0, pair, turn, 0)

    pl.when(y >= 1)(lambda: learn_pair(0))

    def answer(j, carry):
        learn(k_ref[j], v_ref[j], t_ref[j])
        hidden = mm(q_ref[j], half(state_a[...]))
        act = half(hidden * sigmoid(hidden))
        fast = mm(act, half(state_b[...]), NT)
        fast = fast * lax.rsqrt(jnp.mean(fast * fast, axis=1, keepdims=True) + 1e-05)
        heads[j] = half(acc[j] / total[j] + fast * gain_row[...])
        return carry

    for j in range(pair):
        answer(j, 0)

    def ready():
        mine.wait()
        for d in range(1, ways):
            mixing(d).wait_send()
            source = (h - d + ways) % ways
            pltpu.make_async_remote_copy(
                src_ref=mix_ref.at[source], dst_ref=mix_ref.at[source],
                send_sem=mix_send.at[d], recv_sem=mix_recv.at[d],
                device_id=(p, (h + d) % ways), device_id_type=MESH,
            ).wait_recv()

    back = pltpu.make_async_remote_copy(
        src_ref=stage, dst_ref=out_ref.at[plane],
        send_sem=swap_sem.at[0], recv_sem=swap_sem.at[1],
        device_id=(2 * y + 1 - plane, h), device_id_type=MESH,
    )

    def send_back():
        stage[...] = half(mixed[0])
        back.start()

    gather(
        p, h, plane, 1 - plane, False, SPLIT_OUT, heads, held_heads, mix_ref, mixed, ready,
        send_heads, recv_heads, lambda t, chunk, block: None, send_back,
    )
    out_ref[plane] = half(mixed[1])
    back.wait()
    for j in range(pair):
        for which in range(3):
            pl.when(goes_next())(next_copy(j, which).wait_send)
            pl.when(goes_back(j))(back_copy(j, which).wait_send)
            moved = (y == 3) | ((y == 0) & (j == 0)) | ((y == 2) & (j == 1))
            pl.when(moved)(
                outgoing(relayed, j, which, pieces[which][1].at[2, j], y - 1, 1).wait_send
            )


def layer(scale, gain, x, w_in, rate, a0, b0, w_out, collective_id):
    pair, group, width = x.shape
    hid = a0.shape[1]
    ways = lax.axis_size("head")
    ring = lax.axis_size("seq") // 2
    vmem = pl.BlockSpec(memory_space=pltpu.VMEM)
    hbm = pl.BlockSpec(memory_space=pltpu.HBM)
    dma = pltpu.SemaphoreType.DMA
    bf16, f32 = jnp.bfloat16, jnp.float32
    block = pltpu.VMEM((pair, group, width), bf16)
    window = pltpu.VMEM((ring - 1, pair, group, width), bf16)
    return pl.pallas_call(
        layer_kernel,
        out_shape=jax.ShapeDtypeStruct(x.shape, bf16),
        in_specs=[pl.BlockSpec(memory_space=pltpu.SMEM), hbm, hbm, hbm, vmem, hbm, hbm, hbm],
        out_specs=vmem,
        scratch_shapes=[
            pltpu.VMEM((ways, pair, group, width), bf16),
            pltpu.VMEM(w_in.shape, bf16),
            pltpu.VMEM((pair, group, w_in.shape[2]), f32),
            pltpu.VMEM((pair, group, 128), f32),
            block, block, block,
            pltpu.VMEM((pair, 8, group), f32),
            window, window,
            pltpu.VMEM((ring - 1, pair, 8, group), f32),
            pltpu.VMEM((width, hid), f32),
            pltpu.VMEM((width, hid), f32),
            pltpu.VMEM((pair, group, 1), f32),
            pltpu.VMEM((pair, group, 1), f32),
            pltpu.VMEM((pair, group, width), f32),
            pltpu.VMEM((ways, width, width), bf16),
            block,
            pltpu.VMEM((ways, pair, group, width), bf16),
            pltpu.VMEM((pair, group, width), f32),
            pltpu.VMEM((group, width), bf16),
            dma, dma((40 * SPLIT_IN,)), dma((ways, 2, SPLIT_IN)),
            dma((3, pair, 3)), dma((ring - 1, pair, 3)),
            dma((ways,)), dma((ways,)), dma,
            dma((40 * SPLIT_OUT,)), dma((ways, 2, SPLIT_OUT)), dma((2,)),
            pltpu.VMEM(b0.shape, f32), pltpu.VMEM(gain.shape, f32), dma((4,)),
        ],
        compiler_params=pltpu.CompilerParams(
            collective_id=collective_id, has_side_effects=True, vmem_limit_bytes=62 << 20
        ),
        cost_estimate=pl.CostEstimate(
            flops=2 * 10**10, bytes_accessed=10**7, transcendentals=10**6
        ),
    )(scale, gain, x, w_in, rate, a0, b0, w_out)


def gather(
    p, me, plane, first, inward, split, x_ref, held, weights, acc, ready, send_sem, recv_sem, each, middle, swap_sem=None
):
    partner = 2 * (p // 2) + 1 - plane
    x, z, core = me // 4, (me // 2) % 2, me % 2

    def at(dx, dz, dc):
        return ((x + dx + 4) % 4) * 4 + ((z + dz) % 2) * 2 + (core + dc) % 2

    plus, minus, across, twin = at(1, 0, 0), at(-1, 0, 0), at(0, 1, 0), at(0, 0, 1)
    sends = []

    cut = held.shape[2] // split

    def send(chunk, t, target, source=None, parts=range(split)):
        for u in parts:
            rows = pl.ds(u * cut, cut)
            copy = pltpu.make_async_remote_copy(
                src_ref=held.at[chunk, t, rows] if source is None else source.at[rows],
                dst_ref=held.at[chunk, t, rows],
                send_sem=send_sem.at[len(sends)],
                recv_sem=recv_sem.at[chunk, t, u],
                device_id=target, device_id_type=MESH,
            )
            copy.start()
            sends.append(copy)

    def arrived(chunk, t, parts=range(split)):
        for u in parts:
            rows = pl.ds(u * cut, cut)
            pltpu.make_async_remote_copy(
                src_ref=held.at[chunk, t, rows], dst_ref=held.at[chunk, t, rows],
                send_sem=send_sem.at[0], recv_sem=recv_sem.at[chunk, t, u],
                device_id=(p, twin), device_id_type=MESH,
            ).wait_recv()

    if inward:
        send(me, 1, (partner, me), x_ref.at[1 - first])
    for other in (plus, minus, across, twin):
        send(me, 0, (p, other), x_ref.at[first])
    if not inward:
        for other in (minus, plus, across, twin):
            send(me, 1, (p, other), x_ref.at[1 - first])
        held[me, 1] = x_ref[1 - first]
    if inward:
        own = pltpu.make_async_copy(x_ref.at[first], held.at[me, 0], swap_sem)
        own.start()
    else:
        held[me, 0] = x_ref[first]

    acc[...] = jnp.zeros_like(acc)
    ready()

    def take(dx, dz, t, targets):
        chunk = at(dx, dz, 0)
        for u in range(split):
            arrived(chunk, t, (u,))
            for target in targets:
                send(chunk, t, (p, target), None, (u,))
            send(chunk, t, (p, twin), None, (u,))

    def use(dx, dz, t):
        here, there = at(dx, dz, 0), at(dx, dz, 1)
        arrived(there, t)

        def step(i, carry):
            chunk = here + i * (there - here)
            block = held[chunk, t]
            acc[t] += mm(block, weights[chunk])
            each(t, chunk, block)
            return carry

        lax.fori_loop(0, 2, step, 0)

    take(-1, 0, 0, (plus,))
    take(0, 1, 0, (plus, minus))
    take(1, 0, 0, ())
    if inward:
        own.wait()
        for u in range(split):
            arrived(me, 1, (u,))
            for other in (minus, plus, across, twin):
                send(me, 1, (p, other), None, (u,))
    use(0, 0, 0)
    use(-1, 0, 0)
    use(0, 1, 0)
    use(1, 0, 0)
    take(1, 0, 1, (minus,))
    take(0, 1, 1, (minus, plus))
    take(-1, 0, 1, ())
    take(2, 0, 0, (across,))
    use(0, 0, 1)
    use(2, 0, 0)
    take(-1, 1, 0, ())
    take(1, 1, 0, ())
    use(1, 0, 1)
    use(0, 1, 1)
    use(-1, 0, 1)
    take(2, 0, 1, (across,))
    take(2, 1, 0, ())
    use(-1, 1, 0)
    use(1, 1, 0)
    use(2, 1, 0)
    middle()
    use(2, 0, 1)
    take(-1, 1, 1, ())
    take(1, 1, 1, ())
    take(2, 1, 1, ())
    use(-1, 1, 1)
    use(1, 1, 1)
    use(2, 1, 1)
    for copy in sends:
        copy.wait_send()


def body(x, w_in, w_rate, scale, gain, a0, b0, w_out):
    ways = lax.axis_size("head")
    local = x.shape[2]
    w_in = w_in.reshape(ways, local, w_in.shape[2])
    rate = w_rate.astype(jnp.float32).reshape(ways, 1, local)
    return layer(scale, gain, x, w_in, rate, a0[0], b0[0], w_out[0], 1)


def solution(mesh):
    in_specs = (
        P(None, "seq", "head"),
        P(None, "head", None),
        P(None, "head"),
        P("head"),
        P("head", None),
        P("head", None, None),
        P("head", None, None),
        P("head", None, None),
    )
    out_specs = P(None, "seq", "head")
    return jax.shard_map(body, mesh=mesh, in_specs=in_specs, out_specs=out_specs, check_vma=False)
```
